32 devices in a mesh: row: 4 (over z), col: 8 (over y, x, core).
Axes of the slice: x: 2, y: 2, z: 4, core: 2. Of those that a mesh axis runs over, the one named last changes fastest.
Arguments:
- tokens: bfloat16 [1024, 4096], P('row', 'col'), may hold values from -6 to 6
- norm_gain: float32 [4096], replicated, may hold values from 0.1 to 1.9
- expert_ids: int32 [1024, 2], P('row'), may hold values from 0 to 7, all different within a row; in each aligned block of 256 rows (0 to 255, 256 to 511, ...) at most 128 rows name the same one
- gate_weights: float32 [1024, 2], P('row'), may hold values from 0.1 to 1
- w_gate: bfloat16 [8, 4096, 14336], P('row', None, 'col'), may hold values from -0.09375 to 0.09375
- w_up: bfloat16 [8, 4096, 14336], P('row', None, 'col'), may hold values from -0.09375 to 0.09375
- w_down: bfloat16 [8, 14336, 4096], P('row', 'col'), may hold values from -0.046875 to 0.046875
Outputs:
- layer_output: bfloat16 [1024, 4096], P('row', 'col')
The draws below stay inside these ranges and needn't reach their ends.
Inputs may be any that keep to these rules, and one draw needn't show every extreme that they name: `expert_ids`: the 2 experts of a token differ. In each aligned block of 256 tokens no expert is chosen by more than 128 tokens, a bound that some block reaches.
All inputs are finite; a program needn't handle non-finite values.
Results may differ from the reference program's by a relative error of at most 0.0043.
Values may be sent and summed in bfloat16 or wider, within the bound.
No kernel may reach another device: no remote copies, remote signals or barrier semaphores. Data moves between devices by JAX's collectives and lax.ppermute only.
A program may use at most 192 MiB of HBM per device.

```python
import math
import jax
import jax.numpy as jnp
import numpy as np
from jax import lax

D = 4096
FF = 14336
EXPERTS = 8
TOP = 2
TOK_ROW = 256
CAP = 128
TOKENS = 1024


def level_of(key, dims, shards, low, top_value):
    level = 1.0
    for dim, blocks in shards:
        draws = jax.random.uniform(jax.random.fold_in(jax.random.fold_in(key, 6), dim), (blocks,), jnp.float32, low / len(shards), top_value / len(shards))
        level = level * jnp.repeat(jnp.exp(draws), dims[dim] // blocks).reshape((-1,) + (1,) * (len(dims) - 1 - dim))
    return level


def deal_out(rng, own, number, rows, number_of, top, most, skew):
    sequence = jax.random.permutation(rng, number_of)
    packed, common = load_shares(number_of, rows * top, most, skew, True), load_shares(number_of, rows * top, most, skew, False)
    places = jnp.arange(number_of)

    def named(lengths, offset_by):
        used = int((lengths > 0).sum())
        fixed = max(1, used // 4)
        moved = fixed + (places - fixed + offset_by * (used - fixed)) % max(1, number_of - fixed)
        return jnp.zeros((number_of,), jnp.int32).at[sequence[jnp.where(places < fixed, places, moved)]].set(jnp.asarray(lengths, jnp.int32))

    lengths = jnp.where(number % 4 == 0, named(packed, number // 4), named(common, number - number // 4 - 1))
    mixed = jax.random.permutation(jax.random.fold_in(own, 3), number_of)
    donor, sink = mixed[0:number_of // 2 * 2:2], mixed[1:number_of // 2 * 2:2]
    room = jnp.minimum(lengths[donor] - 1, most - lengths[sink]) // 2
    room = jnp.where((donor == sequence[0]) | (sink == sequence[0]) | (lengths[sink] == 0), 0, jnp.maximum(room, 0))
    moved = jax.random.randint(jax.random.fold_in(own, 4), (number_of // 2,), 0, 1 << 20) % (room + 1)
    lengths = lengths.at[donor].add(-moved).at[sink].add(moved)
    items = jnp.searchsorted(jnp.cumsum(lengths), jnp.arange(rows * top), side="right").astype(jnp.int32)
    grid = items.reshape(top, rows).T
    grid = grid[jax.random.permutation(jax.random.fold_in(own, 1), rows)]
    offset_by = jax.random.randint(jax.random.fold_in(own, 2), (rows, 1), 0, top)
    return jnp.take_along_axis(grid, (jnp.arange(top)[None, :] + offset_by) % top, axis=1)


def load_shares(amount, total, bound, lean, full):
    loads = [(1 << 20) // math.isqrt(grade ** lean) + 1 for grade in range(1, amount + 1)]
    largest = bound if full else min(bound, max(-(-total // amount), total * loads[0] // sum(loads)))
    least = 1 if total - largest >= amount - 1 else 0
    holding, rest = [largest] + [least] * (amount - 1), total - largest - least * (amount - 1)
    while rest > 0:
        candidates = [i for i in range(1, amount) if holding[i] < largest] or [i for i in range(1, amount) if holding[i] < bound]
        mass, budget = sum([loads[i] for i in candidates]), rest
        for i in candidates:
            extra = min(bound - holding[i], max(1, budget * loads[i] // mass), rest)
            holding[i] = holding[i] + extra
            rest = rest - extra
    return np.array(holding)


def scatter_about(stream_key, dims, deviation, bound, cuts=(), kind=jnp.bfloat16):
    gain = level_of(stream_key, dims, cuts, -0.22, 0.18) if cuts else 1.0
    array = jax.random.normal(stream_key, dims, jnp.float32) * deviation * gain
    return jnp.minimum(jnp.maximum(array, -bound), bound).astype(kind)


def setup_inputs(seed: int = 0) -> dict:
    splits = jax.random.split(jax.random.key(seed), 8)
    tokens = scatter_about(splits[0], (TOKENS, D), 1.0, 6.0, ((0, 4), (1, 8)))
    norm_gain = jnp.clip(1.0 + 0.18 * jax.random.normal(splits[1], (D,), jnp.float32), 0.1, 1.9)
    expert_ids_keys = jax.random.split(jax.random.fold_in(splits[2], 1), TOKENS // TOK_ROW)
    expert_ids_turns = jax.random.permutation(jax.random.fold_in(splits[2], 3), TOKENS // TOK_ROW)
    expert_ids = jax.vmap(lambda own, number: deal_out(jax.random.fold_in(splits[2], 2), own, number, TOK_ROW, EXPERTS, TOP, CAP, 2))(expert_ids_keys, expert_ids_turns).reshape((TOKENS, TOP))
    gate_weights = jnp.clip(0.1 + 0.9 * jax.random.uniform(splits[3], (TOKENS, TOP), jnp.float32) ** level_of(splits[3], (TOKENS, TOP), ((0, 4),), -0.2, 0.2), 0.1, 1.0)
    w_gate = scatter_about(splits[4], (EXPERTS, D, FF), D ** -0.5, 0.09375, ((0, 4), (2, 8)))
    w_up = scatter_about(splits[5], (EXPERTS, D, FF), D ** -0.5, 0.09375, ((0, 4), (2, 8)))
    w_down = scatter_about(splits[6], (EXPERTS, FF, D), FF ** -0.5, 0.046875, ((0, 4), (1, 8)))
    return {"tokens": tokens, "norm_gain": norm_gain, "expert_ids": expert_ids, "gate_weights": gate_weights, "w_gate": w_gate, "w_up": w_up, "w_down": w_down}


def normalize(rows, norm_gain):
    values = rows.astype(jnp.float32)
    inverse_norm = lax.rsqrt(lax.optimization_barrier(jnp.mean(values * values, axis=-1, keepdims=True)) + 1e-05)
    return (values * inverse_norm * norm_gain.astype(jnp.float32)).astype(jnp.bfloat16)

def reference(tokens, norm_gain, expert_ids, gate_weights, w_gate, w_up, w_down):
    normed = normalize(tokens, norm_gain)
    flat_ids = expert_ids.reshape(-1).astype(jnp.int32)
    flat_gates = gate_weights.reshape(-1).astype(jnp.float32)
    token_count = tokens.shape[0]
    limit = TOKENS // 2
    owner_ids = (jnp.arange(flat_ids.shape[0], dtype=jnp.int32) // TOP).astype(jnp.int32)

    def one_expert(index, total):
        expert_hits = (flat_ids == index).astype(jnp.int32)
        ranks = (jnp.cumsum(expert_hits) - expert_hits).astype(jnp.int32)
        targets = jnp.where(expert_hits > 0, ranks, limit).astype(jnp.int32)
        owners = jnp.zeros((limit,), jnp.int32).at[targets].set(owner_ids, mode='drop')
        gathered = normed[owners]
        gate_part = jnp.dot(gathered, w_gate[index], preferred_element_type=jnp.float32)
        up_part = jnp.dot(gathered, w_up[index], preferred_element_type=jnp.float32)
        hidden = (jax.nn.silu(gate_part) * up_part).astype(jnp.bfloat16)
        outputs = jnp.dot(hidden, w_down[index], preferred_element_type=jnp.float32)
        picked = outputs[jnp.minimum(ranks, limit - 1)]
        scaled = picked * (flat_gates * expert_hits.astype(jnp.float32))[:, None]
        return total + lax.optimization_barrier(jnp.sum(scaled.reshape(token_count, TOP, -1), axis=1))
    mixed = lax.fori_loop(0, EXPERTS, one_expert, jnp.zeros(tokens.shape, jnp.float32))
    return (tokens.astype(jnp.float32) + mixed).astype(jnp.bfloat16)
```

```python
import functools
import jax
import jax.numpy as jnp
from jax import lax
from jax.experimental import pallas as pl
from jax.experimental.pallas import tpu as pltpu
from jax.sharding import PartitionSpec as P

EXPERTS = 8
CAP = 128
WINDOW = 6
F32 = jnp.float32
BF16 = jnp.bfloat16
MIB = 1024 * 1024


def pack_kernel(local, ids_ref, tokens_ref, *out_refs):
    tokens = tokens_ref.shape[0]
    lanes = lax.broadcasted_iota(jnp.int32, (tokens, 128), 1)
    first, second = ids_ref[:, 0:1], ids_ref[:, 1:2]
    hits = jnp.where((lanes == first) | (lanes == second), 1.0, 0.0)
    hits_t = jnp.transpose(hits)[0:EXPERTS, :]
    before = lax.broadcasted_iota(jnp.int32, (tokens, tokens), 0)
    after = lax.broadcasted_iota(jnp.int32, (tokens, tokens), 1)
    upper = jnp.where(before < after, 1.0, 0.0).astype(BF16)
    ranks_t = jnp.dot(hits_t.astype(BF16), upper, preferred_element_type=F32)
    slots = lax.broadcasted_iota(jnp.int32, (CAP, tokens), 0).astype(F32)
    for expert in range(EXPERTS):
        rank, hit = ranks_t[expert : expert + 1, :], hits_t[expert : expert + 1, :]
        picker = jnp.where((slots == rank) & (hit > 0.0), 1.0, 0.0).astype(BF16)
        rows = jnp.dot(picker, tokens_ref[...], preferred_element_type=F32)
        out_refs[expert // local][expert % local] = rows.astype(BF16)


def pack(relative_ids, tokens, rows, local):
    width = tokens.shape[1]
    return pl.pallas_call(
        functools.partial(pack_kernel, local),
        out_shape=[jax.ShapeDtypeStruct((local, CAP, width), BF16)] * rows,
        compiler_params=pltpu.CompilerParams(vmem_limit_bytes=32 * MIB),
        name="pack",
    )(relative_ids, tokens)


def combine_kernel(ids_ref, weights_ref, tokens_ref, *refs):
    slot_refs, out_ref = refs[:-1], refs[-1]
    tokens = tokens_ref.shape[0]
    lanes = lax.broadcasted_iota(jnp.int32, (tokens, 128), 1)
    first, second = ids_ref[:, 0:1], ids_ref[:, 1:2]
    hits = jnp.where((lanes == first) | (lanes == second), 1.0, 0.0)
    row = lax.broadcasted_iota(jnp.int32, (tokens, tokens), 0)
    column = lax.broadcasted_iota(jnp.int32, (tokens, tokens), 1)
    lower = jnp.where(column < row, 1.0, 0.0).astype(BF16)
    ranks = jnp.dot(lower, hits.astype(BF16), preferred_element_type=F32)
    total = tokens_ref[...].astype(F32)
    for choice, ids in enumerate((first, second)):
        rank = jnp.sum(jnp.where(lanes == ids, ranks, 0.0), axis=1, keepdims=True)
        matches = jnp.where(lanes.astype(F32) == rank, 1.0, 0.0)
        picked = jnp.zeros(total.shape, F32)
        for expert, slot_ref in enumerate(slot_refs):
            picker = jnp.where(ids == expert, matches, 0.0).astype(BF16)
            picked += jnp.dot(picker, slot_ref[...], preferred_element_type=F32)
        total += picked * weights_ref[:, choice : choice + 1]
    out_ref[...] = total.astype(BF16)


def combine(relative_ids, gate_weights, tokens, slots):
    return pl.pallas_call(
        combine_kernel,
        out_shape=jax.ShapeDtypeStruct(tokens.shape, BF16),
        compiler_params=pltpu.CompilerParams(vmem_limit_bytes=32 * MIB),
        name="combine",
    )(relative_ids, gate_weights, tokens, *slots)


def ffn_kernel(expert, blocks, cols, place_ref, gain_ref, *refs):
    pieces = refs[: blocks * cols]
    w_gate, w_up, w_down, send_out, keep_out = refs[blocks * cols : blocks * cols + 5]
    raw, normed, gates, ups, downs, hidden, staged = refs[blocks * cols + 5 : blocks * cols + 12]
    x_sem, gate_sem, up_sem, down_sem, out_sem = refs[blocks * cols + 12 :]
    tiles, _, tile = gates.shape
    width = downs.shape[2]
    place = place_ref[0]

    def group(step):
        return jnp.bitwise_xor(place, jnp.where(step < cols // 2, 2 * step + 1, 2 * step - cols))

    copies = []
    for block in range(blocks):
        for relative in range(cols):
            at = pl.multiple_of(jnp.bitwise_xor(place, relative) * width, width)
            copies.append(
                pltpu.make_async_copy(
                    pieces[block * cols + relative].at[expert],
                    raw.at[pl.ds(block * CAP, CAP), pl.ds(at, width)],
                    x_sem.at[block * cols + relative],
                )
            )

    def gate_copy(index):
        columns = pl.ds(pl.multiple_of(index * tile, tile), tile)
        return pltpu.make_async_copy(
            w_gate.at[expert, :, columns], gates.at[index], gate_sem.at[index]
        )

    def up_copy(index):
        columns = pl.ds(pl.multiple_of(index * tile, tile), tile)
        return pltpu.make_async_copy(w_up.at[expert, :, columns], ups.at[index], up_sem.at[index])

    def down_copy(index):
        columns = pl.ds(pl.multiple_of(group(index) * width, width), width)
        return pltpu.make_async_copy(
            w_down.at[expert, :, columns], downs.at[index], down_sem.at[index]
        )

    jobs = []
    for index in range(tiles):
        jobs += [gate_copy(index), up_copy(index)]
    jobs += [down_copy(index) for index in range(cols)]

    for copy in copies:
        copy.start()
    for job in jobs[:WINDOW]:
        job.start()
    for copy in copies:
        copy.wait()
    values = raw[...].astype(F32)
    features = raw.shape[1]
    mean = jnp.sum(values * values, axis=1, keepdims=True) * (1.0 / features)
    normed[...] = (values * lax.rsqrt(mean + 1e-05) * gain_ref[...]).astype(BF16)

    def finish(index):
        jobs[index].wait()
        if index + WINDOW < len(jobs):
            jobs[index + WINDOW].start()

    for index in range(tiles):
        finish(2 * index)
        gate = jnp.dot(normed[...], gates[index], preferred_element_type=F32)
        finish(2 * index + 1)
        up = jnp.dot(normed[...], ups[index], preferred_element_type=F32)
        hidden[:, index * tile : (index + 1) * tile] = (
            gate / (1.0 + jnp.exp(-gate)) * up
        ).astype(BF16)

    outs = []
    for index in range(cols):
        finish(2 * tiles + index)
        staged[index] = jnp.dot(
            hidden[...], downs[index], preferred_element_type=F32
        ).astype(BF16)
        half = cols // 2
        target = send_out.at[index] if index < half else keep_out.at[index - half]
        out = pltpu.make_async_copy(staged.at[index], target, out_sem.at[index])
        out.start()
        outs.append(out)
    for out in outs:
        out.wait()


def ffn(expert, pieces, place, norm_gain, w_gate, w_up, w_down):
    blocks, cols = len(pieces), len(pieces[0])
    features, units = w_gate.shape[1], w_gate.shape[2]
    width, rows = features // cols, blocks * CAP
    tile = 256 if units % 256 == 0 else 128
    tiles = units // tile
    anywhere = pl.BlockSpec(memory_space=pl.ANY)
    flat = [piece for block in pieces for piece in block]
    half = jax.ShapeDtypeStruct((cols // 2, rows, width), BF16)
    weights = 3 * features * units
    return pl.pallas_call(
        functools.partial(ffn_kernel, expert, blocks, cols),
        out_shape=[half, half],
        in_specs=[
            pl.BlockSpec(memory_space=pltpu.SMEM),
            pl.BlockSpec(memory_space=pltpu.VMEM),
        ]
        + [anywhere] * (len(flat) + 3),
        out_specs=[anywhere, anywhere],
        scratch_shapes=[
            pltpu.VMEM((rows, features), BF16),
            pltpu.VMEM((rows, features), BF16),
            pltpu.VMEM((tiles, features, tile), BF16),
            pltpu.VMEM((tiles, features, tile), BF16),
            pltpu.VMEM((cols, units, width), BF16),
            pltpu.VMEM((rows, units), BF16),
            pltpu.VMEM((cols, rows, width), BF16),
            pltpu.SemaphoreType.DMA((len(flat),)),
            pltpu.SemaphoreType.DMA((tiles,)),
            pltpu.SemaphoreType.DMA((tiles,)),
            pltpu.SemaphoreType.DMA((cols,)),
            pltpu.SemaphoreType.DMA((cols,)),
        ],
        compiler_params=pltpu.CompilerParams(vmem_limit_bytes=58 * MIB),
        cost_estimate=pl.CostEstimate(
            flops=2 * rows * weights, bytes_accessed=2 * weights, transcendentals=rows * units
        ),
        name="ffn",
    )(place, norm_gain.reshape(1, features), *flat, w_gate, w_up, w_down)


def body(rows, cols, tokens, norm_gain, expert_ids, gate_weights, w_gate, w_up, w_down):
    local = EXPERTS // rows
    row, place = lax.axis_index("row"), lax.axis_index("col").reshape(1)

    def along_row(value, relative):
        if relative == 0:
            return value
        return lax.ppermute(value, "row", [(i, i ^ relative) for i in range(rows)])

    def along_col(value, relative):
        if relative == 0:
            return value
        return lax.ppermute(value, "col", [(i, i ^ relative) for i in range(cols)])

    relative_ids = jnp.bitwise_xor(expert_ids, row * local)
    packed = pack(relative_ids, tokens, rows, local)
    arrived = [along_row(packed[k], k) for k in range(rows)]

    def gather(shares):
        same_core = [along_col(shares, q) for q in range(0, cols, 2)]
        other_core = [along_col(piece, 1) for piece in same_core]
        return [piece for pair in zip(same_core, other_core) for piece in pair]

    pieces = [gather(arrived[k]) for k in range(rows)]
    returned = [[None] * local for _ in range(rows)]
    for first in range(0, rows, 2):
        for expert in range(local):
            group = pieces[first : first + 2]
            send, keep = ffn(expert, group, place, norm_gain, w_gate, w_up, w_down)
            got = along_col(send, 1)
            pair = [
                (keep[q].astype(F32) + got[q].astype(F32)).astype(BF16) for q in range(cols // 2)
            ]
            total = pair[0].astype(F32)
            for q in range(1, cols // 2):
                total += along_col(pair[q], 2 * q).astype(F32)
            total = total.astype(BF16)
            for block in range(2):
                share = total[block * CAP : (block + 1) * CAP]
                returned[first + block][expert] = along_row(share, first + block)
    slots = [share for shares in returned for share in shares]
    return combine(relative_ids, gate_weights, tokens, slots)


def solution(mesh):
    placed = (
        P("row", "col"),
        P(),
        P("row", None),
        P("row", None),
        P("row", None, "col"),
        P("row", None, "col"),
        P("row", "col", None),
    )
    return jax.shard_map(
        functools.partial(body, mesh.shape["row"], mesh.shape["col"]),
        mesh=mesh,
        in_specs=placed,
        out_specs=P("row", "col"),
        check_vma=False,
    )
```

```python
import functools
import jax
import jax.numpy as jnp
from jax import lax
from jax.experimental import pallas as pl
from jax.experimental.pallas import tpu as pltpu
from jax.sharding import PartitionSpec as P

EXPERTS = 8
CAP = 128
SLOTS = 3
F32 = jnp.float32
BF16 = jnp.bfloat16
VMEM = 64 * 1024 * 1024


def pack_kernel(chosen, base_ref, ids_ref, tokens_ref, *out_refs):
    tokens = tokens_ref.shape[0]
    numbers = lax.broadcasted_iota(jnp.int32, (EXPERTS, tokens), 0)
    ids = jnp.bitwise_xor(ids_ref[...], base_ref[0])
    hit = (numbers == ids[0:1, :]) | (numbers == ids[1:2, :])
    hits = jnp.where(hit, 1.0, 0.0)
    before = lax.broadcasted_iota(jnp.int32, (tokens, tokens), 0)
    after = lax.broadcasted_iota(jnp.int32, (tokens, tokens), 1)
    upper = jnp.where(before < after, 1.0, 0.0).astype(BF16)
    ranks = jnp.dot(hits.astype(BF16), upper, preferred_element_type=F32)
    ranks = jnp.where(hit, ranks, -1.0)
    slots = lax.broadcasted_iota(jnp.int32, (CAP, tokens), 0).astype(F32)
    for out_ref, experts in zip(out_refs, chosen):
        for index, expert in enumerate(experts):
            picker = jnp.where(slots == ranks[expert : expert + 1, :], 1.0, 0.0).astype(BF16)
            rows = jnp.dot(picker, tokens_ref[...], preferred_element_type=F32)
            out_ref[index] = rows.astype(BF16)


def pack(chosen, base, ids, tokens):
    width = tokens.shape[1]
    vmem = pl.BlockSpec(memory_space=pltpu.VMEM)
    return pl.pallas_call(
        functools.partial(pack_kernel, chosen),
        out_shape=[jax.ShapeDtypeStruct((len(c), CAP, width), BF16) for c in chosen],
        in_specs=[pl.BlockSpec(memory_space=pltpu.SMEM), vmem, vmem],
        out_specs=[vmem] * len(chosen),
        compiler_params=pltpu.CompilerParams(vmem_limit_bytes=VMEM),
        name="pack",
    )(base, ids, tokens)


def stack_kernel(layout, count, *refs):
    sources, out_refs = refs[:count], refs[-len(layout) :]
    for out_ref, parts in zip(out_refs, layout):
        for index, (source, at) in enumerate(parts):
            out_ref[index] = sources[source][at]


def stack(layout, sources, token=None):
    tokens = () if token is None else (token,)
    vmem = pl.BlockSpec(memory_space=pltpu.VMEM)
    block = sources[0].shape[1:]
    return pl.pallas_call(
        functools.partial(stack_kernel, layout, len(sources)),
        out_shape=[jax.ShapeDtypeStruct((len(parts),) + block, BF16) for parts in layout],
        in_specs=[vmem] * len(sources) + [pl.BlockSpec(memory_space=pltpu.SMEM)] * len(tokens),
        out_specs=[vmem] * len(layout),
        compiler_params=pltpu.CompilerParams(vmem_limit_bytes=VMEM),
        name="stack",
    )(*sources, *tokens)


def combine_kernel(experts, base_ref, ids_ref, weights_ref, start_ref, *refs):
    slot_refs, out_ref = refs[:-1], refs[-1]
    tokens = start_ref.shape[0]
    ids = jnp.bitwise_xor(ids_ref[...], base_ref[0]).astype(F32)
    filler = jnp.zeros((4, tokens), F32)
    columns = jnp.transpose(jnp.concatenate([ids, weights_ref[...], filler], axis=0))
    lanes = lax.broadcasted_iota(jnp.int32, (tokens, 128), 1).astype(F32)
    first, second = columns[:, 0:1], columns[:, 1:2]
    hits = jnp.where((lanes == first) | (lanes == second), 1.0, 0.0)
    row = lax.broadcasted_iota(jnp.int32, (tokens, tokens), 0)
    column = lax.broadcasted_iota(jnp.int32, (tokens, tokens), 1)
    lower = jnp.where(column < row, 1.0, 0.0).astype(BF16)
    ranks = jnp.dot(lower, hits.astype(BF16), preferred_element_type=F32)
    total = start_ref[...].astype(F32)
    for choice, chosen in enumerate((first, second)):
        rank = jnp.sum(jnp.where(lanes == chosen, ranks, 0.0), axis=1, keepdims=True)
        matches = jnp.where(lanes == rank, 1.0, 0.0)
        picked = jnp.zeros(total.shape, F32)
        for expert, slot_ref in zip(experts, slot_refs):
            picker = jnp.where(chosen == expert, matches, 0.0).astype(BF16)
            picked += jnp.dot(picker, slot_ref[...], preferred_element_type=F32)
        total += picked * columns[:, 2 + choice : 3 + choice]
    out_ref[...] = total.astype(out_ref.dtype)


def combine(experts, base, ids, gate_weights, start, slots, kind):
    vmem = pl.BlockSpec(memory_space=pltpu.VMEM)
    return pl.pallas_call(
        functools.partial(combine_kernel, experts),
        out_shape=jax.ShapeDtypeStruct(start.shape, kind),
        in_specs=[pl.BlockSpec(memory_space=pltpu.SMEM)] + [vmem] * (3 + len(slots)),
        out_specs=vmem,
        compiler_params=pltpu.CompilerParams(vmem_limit_bytes=VMEM),
        name="combine",
    )(base, ids, gate_weights, start, *slots)


def up_kernel(expert, blocks, cols, places, place_ref, gain_ref, *refs):
    count = blocks * cols
    pieces = refs[:count]
    w_gate, w_up, w_down = refs[count : count + 3]
    (send_out, early_out, hidden_out, done_out, raw, scaled, ups, downs, hidden, staged, total, squares) = refs[-18:-6]
    x_sem, gate_sem, up_sem, down_sem, out_sem, hidden_sem = refs[-6:]
    slots, features = ups.shape[0], ups.shape[1]
    tile, units, width = ups.shape[2] // 2, hidden.shape[1], raw.shape[2]
    tiles, half = units // tile, cols // 2
    place = place_ref[0]
    done_out[0] = place

    def up_copies(index):
        slot = lax.rem(index, slots)
        columns = pl.ds(pl.multiple_of(index * tile, tile), tile)
        return (
            pltpu.make_async_copy(
                w_gate.at[expert, :, columns], ups.at[slot, :, pl.ds(0, tile)], gate_sem.at[slot]
            ),
            pltpu.make_async_copy(
                w_up.at[expert, :, columns], ups.at[slot, :, pl.ds(tile, tile)], up_sem.at[slot]
            ),
        )

    def down_copy(index):
        core, at = (1, index) if index < half else (0, index - half)
        return down_piece(expert, w_down, downs, down_sem, place, index, at, core)

    def piece_copies(relative):
        copies = []
        for block in range(blocks):
            number = block * cols + relative
            piece, at = pieces[number], places[number]
            if len(piece.shape) == 4:
                source = piece.at[jnp.bitwise_xor(place, relative), at]
            else:
                source = piece.at[at]
            target = raw.at[relative, pl.ds(block * CAP, CAP), :]
            copies.append(pltpu.make_async_copy(source, target, x_sem.at[number]))
        return copies

    for relative in range(cols):
        for copy in piece_copies(relative):
            copy.start()
    for copy in up_copies(0):
        copy.start()
    for relative in range(cols):
        for copy in piece_copies(relative):
            copy.wait()
        if relative == 0:
            for copy in up_copies(0):
                copy.wait()
            for index in range(1, slots):
                for copy in up_copies(index):
                    copy.start()
        owner = jnp.bitwise_xor(place, relative)
        at = pl.ds(pl.multiple_of(owner * width, width), width)
        values = raw[relative].astype(F32)
        square = values * values
        part = square[:, 0:128]
        for lane in range(128, width, 128):
            part += square[:, lane : lane + 128]
        share = (values * gain_ref[owner]).astype(BF16)
        scaled[:, at] = share
        product = jnp.dot(share, ups[0, at, :], preferred_element_type=F32)
        if relative == 0:
            squares[...] = part
            total[...] = product
        else:
            squares[...] += part
            total[...] += product
    mean = jnp.sum(squares[...], axis=1, keepdims=True) * (1.0 / features)
    squares[...] = jnp.broadcast_to(lax.rsqrt(mean + 1e-05), squares.shape)

    def activate(both, columns):
        inverse = squares[:, 0:1]
        gate, up = both[:, :tile] * inverse, both[:, tile:] * inverse
        hidden[:, columns] = (gate / (1.0 + jnp.exp(-gate)) * up).astype(BF16)

    activate(total[...], pl.ds(0, tile))

    @pl.loop(1, tiles)
    def _(index):
        for copy in up_copies(index):
            copy.wait()

        @pl.when(index + slots - 1 < tiles)
        def _():
            for copy in up_copies(index + slots - 1):
                copy.start()

        for step in range(half + half // 2):

            @pl.when(index == tiles - slots + 1 + step * (slots - 1) // (half + half // 2))
            def _():
                down_copy(step).start()

        both = jnp.dot(scaled[...], ups[lax.rem(index, slots)], preferred_element_type=F32)
        activate(both, pl.ds(pl.multiple_of(index * tile, tile), tile))

    hidden_copy = pltpu.make_async_copy(hidden, hidden_out, hidden_sem)
    hidden_copy.start()
    targets = [send_out.at[index] for index in range(half)]
    targets += [early_out.at[index] for index in range(half // 2)]
    finish_down(targets, hidden, downs, staged, down_copy, out_sem)
    hidden_copy.wait()


def down_piece(expert, w_down, downs, down_sem, place, slot, index, core):
    width = downs.shape[2] // 2
    owner = jnp.bitwise_xor(place, 2 * index + core)
    return pltpu.make_async_copy(
        w_down.at[expert, :, pl.ds(pl.multiple_of(owner * width, width), width)],
        downs.at[slot // 2, :, pl.ds(slot % 2 * width, width)],
        down_sem.at[slot],
    )


def finish_down(targets, hidden, downs, staged, down_copy, out_sem):
    outs = []
    width = downs.shape[2] // 2
    for index in range(0, len(targets), 2):
        down_copy(index).wait()
        down_copy(index + 1).wait()
        both = jnp.dot(hidden[...], downs[index // 2], preferred_element_type=F32).astype(BF16)
        for at in (index, index + 1):
            start = (at - index) * width
            staged[at] = both[:, start : start + width]
            outs.append(pltpu.make_async_copy(staged.at[at], targets[at], out_sem.at[at]))
            outs[-1].start()
    for out in outs:
        out.wait()


def down_kernel(expert, count, place_ref, hidden_ref, w_down, *refs):
    terms = refs[:count]
    hidden, downs, staged, down_sem, out_sem, hidden_sem = refs[-6:]
    late = staged.shape[0]

    def down_copy(index):
        return down_piece(expert, w_down, downs, down_sem, place_ref[0], index, late + index, 0)

    hidden_copy = pltpu.make_async_copy(hidden_ref, hidden, hidden_sem)
    hidden_copy.start()
    if count:
        late_out, low_out, high_out, held, summed, term_sem, sum_sem = refs[-13:-6]
        copies = [
            pltpu.make_async_copy(terms[index], held.at[index], term_sem.at[index])
            for index in range(count)
        ]
        for copy in copies:
            copy.start()
    else:
        late_out = refs[-7]
    for index in range(late):
        down_copy(index).start()
    outs = []
    if count:
        for copy in copies:
            copy.wait()
        total = held[0].astype(F32)
        for index in range(1, count):
            total += held[index].astype(F32)
        summed[...] = total.astype(BF16)
        for index, out_ref in enumerate((low_out, high_out)):
            rows = pl.ds(index * CAP, CAP)
            outs.append(pltpu.make_async_copy(summed.at[rows], out_ref, sum_sem.at[index]))
            outs[-1].start()
    hidden_copy.wait()
    targets = [late_out.at[index] for index in range(late)]
    finish_down(targets, hidden, downs, staged, down_copy, out_sem)
    for out in outs:
        out.wait()


def expand(expert, pieces, place, norm_gain, w_gate, w_up, w_down, after=()):
    blocks, cols = len(pieces), len(pieces[0])
    features, units = w_gate.shape[1], w_gate.shape[2]
    width, rows, half = features // cols, blocks * CAP, cols // 2
    tile = 256 if units % 256 == 0 else 128
    anywhere = pl.BlockSpec(memory_space=pl.ANY)
    flat = [array for block in pieces for array, _ in block]
    places = [index for block in pieces for _, index in block]
    downs = half + half // 2
    weights = 2 * features * units + downs * units * width
    return pl.pallas_call(
        functools.partial(up_kernel, expert, blocks, cols, places),
        out_shape=[
            jax.ShapeDtypeStruct((half, rows, width), BF16),
            jax.ShapeDtypeStruct((half // 2, rows, width), BF16),
            jax.ShapeDtypeStruct((rows, units), BF16),
            jax.ShapeDtypeStruct((1,), jnp.int32),
        ],
        in_specs=[
            pl.BlockSpec(memory_space=pltpu.SMEM),
            pl.BlockSpec(memory_space=pltpu.VMEM),
        ]
        + [anywhere] * (len(flat) + 3 + len(after)),
        out_specs=[anywhere, anywhere, anywhere, pl.BlockSpec(memory_space=pltpu.SMEM)],
        scratch_shapes=[
            pltpu.VMEM((cols, rows, width), BF16),
            pltpu.VMEM((rows, features), BF16),
            pltpu.VMEM((SLOTS, features, 2 * tile), BF16),
            pltpu.VMEM((downs // 2, units, 2 * width), BF16),
            pltpu.VMEM((rows, units), BF16),
            pltpu.VMEM((downs, rows, width), BF16),
            pltpu.VMEM((rows, 2 * tile), F32),
            pltpu.VMEM((rows, 128), F32),
            pltpu.SemaphoreType.DMA((len(flat),)),
            pltpu.SemaphoreType.DMA((SLOTS,)),
            pltpu.SemaphoreType.DMA((SLOTS,)),
            pltpu.SemaphoreType.DMA((downs,)),
            pltpu.SemaphoreType.DMA((downs,)),
            pltpu.SemaphoreType.DMA,
        ],
        compiler_params=pltpu.CompilerParams(vmem_limit_bytes=VMEM),
        cost_estimate=pl.CostEstimate(
            flops=2 * rows * weights, bytes_accessed=2 * weights, transcendentals=rows * units
        ),
        name="expand",
    )(place, norm_gain.reshape(cols, 1, width), *flat, w_gate, w_up, w_down, *after)


def contract(expert, hidden, cols, place, w_down, terms=(), after=()):
    rows, units = hidden.shape
    width, late, count = w_down.shape[2] // cols, cols // 4, len(terms)
    anywhere = pl.BlockSpec(memory_space=pl.ANY)
    weights = units * width * late
    block = jax.ShapeDtypeStruct((CAP, width), BF16)
    side = [
        pltpu.VMEM((count, rows, width), BF16),
        pltpu.VMEM((rows, width), BF16),
        pltpu.SemaphoreType.DMA((count,)),
        pltpu.SemaphoreType.DMA((2,)),
    ]
    out_shape = [jax.ShapeDtypeStruct((late, rows, width), BF16)] + [block, block] * bool(count)
    return pl.pallas_call(
        functools.partial(down_kernel, expert, count),
        out_shape=out_shape,
        in_specs=[pl.BlockSpec(memory_space=pltpu.SMEM)] + [anywhere] * (2 + count + len(after)),
        out_specs=[anywhere] * len(out_shape),
        scratch_shapes=side * bool(count)
        + [
            pltpu.VMEM((rows, units), BF16),
            pltpu.VMEM((late // 2, units, 2 * width), BF16),
            pltpu.VMEM((late, rows, width), BF16),
            pltpu.SemaphoreType.DMA((late,)),
            pltpu.SemaphoreType.DMA((late,)),
            pltpu.SemaphoreType.DMA,
        ],
        compiler_params=pltpu.CompilerParams(vmem_limit_bytes=VMEM),
        cost_estimate=pl.CostEstimate(
            flops=128 * rows * weights, bytes_accessed=128 * weights, transcendentals=0
        ),
        name="contract",
    )(place, hidden, w_down, *terms, *after)


def pair_kernel(early_ref, late_ref, other_ref, *refs):
    half = other_ref.shape[0]
    out_refs = refs[:half]
    mine, other, staged, mine_sem, other_sem, out_sem = refs[half:]
    copies = []
    for index in range(half):
        source, at = (early_ref, index) if index < half // 2 else (late_ref, index - half // 2)
        copies.append(
            (
                pltpu.make_async_copy(source.at[at], mine.at[index], mine_sem.at[index]),
                pltpu.make_async_copy(other_ref.at[index], other.at[index], other_sem.at[index]),
            )
        )
    for ours, theirs in copies:
        ours.start()
        theirs.start()
    outs = []
    for index in range(half):
        for copy in copies[index]:
            copy.wait()
        both = mine[index].astype(F32) + other[index].astype(F32)
        staged[index] = both.astype(BF16)
        outs.append(pltpu.make_async_copy(staged.at[index], out_refs[index], out_sem.at[index]))
        outs[-1].start()
    for out in outs:
        out.wait()


def pair_sums(early, late, other):
    half, block = other.shape[0], other.shape[1:]
    anywhere = pl.BlockSpec(memory_space=pl.ANY)
    return pl.pallas_call(
        pair_kernel,
        out_shape=[jax.ShapeDtypeStruct(block, BF16)] * half,
        in_specs=[anywhere] * 3,
        out_specs=[anywhere] * half,
        scratch_shapes=[pltpu.VMEM(other.shape, BF16)] * 3 + [pltpu.SemaphoreType.DMA((half,))] * 3,
        compiler_params=pltpu.CompilerParams(vmem_limit_bytes=VMEM),
        name="pair_sums",
    )(early, late, other)


def add_kernel(count, *refs):
    terms, out_refs = refs[:count], refs[-2:]
    total = terms[0][...].astype(F32)
    for term in terms[1:]:
        total += term[...].astype(F32)
    for index, out_ref in enumerate(out_refs):
        out_ref[...] = total[index * CAP : (index + 1) * CAP].astype(BF16)


def add(terms):
    vmem = pl.BlockSpec(memory_space=pltpu.VMEM)
    block = jax.ShapeDtypeStruct((CAP, terms[0].shape[1]), BF16)
    return pl.pallas_call(
        functools.partial(add_kernel, len(terms)),
        out_shape=[block, block],
        in_specs=[vmem] * len(terms),
        out_specs=[vmem, vmem],
        compiler_params=pltpu.CompilerParams(vmem_limit_bytes=VMEM),
        name="add",
    )(*terms)


def body(rows, cols, tokens, norm_gain, expert_ids, gate_weights, w_gate, w_up, w_down):
    local = EXPERTS // rows
    half = cols // 2
    row, place = lax.axis_index("row"), lax.axis_index("col").reshape(1)

    def along_row(value, relative):
        if relative == 0:
            return value
        return lax.ppermute(value, "row", [(i, i ^ relative) for i in range(rows)])

    def along_col(value, relative):
        if relative == 0:
            return value
        return lax.ppermute(value, "col", [(i, i ^ relative) for i in range(cols)])

    def gather(shares):
        return [along_col(shares, q) for q in range(0, cols, 2)]

    def complete(same_core):
        other_core = [along_col(piece, 1) for piece in same_core]
        return [piece for pair in zip(same_core, other_core) for piece in pair]

    def blocks_of(pieces):
        return [[(p, block) for p in pieces] for block in range(2)]

    base = (row * local).reshape(1)
    ids, token_weights = expert_ids.T, gate_weights.T
    blocks = [(k, k + 1) for k in range(0, rows, 2)]
    experts = range(local)
    chosen = [[k * local + e] for k in range(2) for e in experts]
    chosen += [[k * local + e for e in experts] for k in range(2, rows)]
    packed = pack(chosen, base, ids, tokens)
    own, sent, far = packed[:local], packed[local : 2 * local], packed[2 * local :]
    near = [along_row(share, 1) for share in sent]
    shares = stack([[(0, 0), (1, 0)]], [own[0], near[0]])[0]
    first_pieces = blocks_of(complete(gather(shares)))
    gathered = {}
    stacked = []
    for e in experts[1:]:
        stacked += stack([[(0, 0), (1, 0)]], [own[e], near[e]])
        gathered[(0, e)] = lax.all_gather(stacked[-1], "col", axis=0)
    arrived = {k: along_row(far[k - 2], k) for k in range(2, rows)}

    order = [(index, e) for index in range(len(blocks)) for e in experts]
    returned = {}
    terms, home, pairs = (), [], stacked
    for position, (index, e) in enumerate(order):
        if position == 0:
            pieces = first_pieces
        elif index == 0:
            pieces = [[(gathered[(0, e)], block)] * cols for block in range(2)]
        else:
            pieces = [[(gathered[index], e * 2 + block)] * cols for block in range(2)]
        send, early, hidden, done = expand(
            e, pieces, place, norm_gain, w_gate, w_up, w_down, after=pairs
        )
        after = list(home)
        if position == 0:
            for other, ks in enumerate(blocks[1:], 1):
                layout = [[(source, e_) for e_ in experts for source in range(2)]]
                shares = stack(layout, [arrived[k] for k in ks], token=done)[0]
                gathered[other] = lax.all_gather(shares, "col", axis=0)
                after.append(shares)
        got = along_col(send, 1)
        late, *totals = contract(e, hidden, cols, place, w_down, terms=terms, after=after)
        home = []
        if totals:
            index_, e_ = order[position - 1]
            for k, total in zip(blocks[index_], totals):
                returned[k * local + e_] = along_row(total, k)
                home.append(returned[k * local + e_])
        pairs = pair_sums(early, late, got)
        terms = [along_col(share, 2 * q) for q, share in enumerate(pairs)]
    numbers = sorted(returned)
    slots = [returned[number] for number in numbers]
    partial = combine(numbers, base, ids, token_weights, tokens, slots, F32)
    index, e = order[-1]
    numbers = [k * local + e for k in blocks[index]]
    slots = [along_row(total, k) for k, total in zip(blocks[index], add(terms))]
    return combine(numbers, base, ids, token_weights, partial, slots, BF16)


def solution(mesh):
    placed = (
        P("row", "col"),
        P(),
        P("row", None),
        P("row", None),
        P("row", None, "col"),
        P("row", None, "col"),
        P("row", "col", None),
    )
    return jax.shard_map(
        functools.partial(body, mesh.shape["row"], mesh.shape["col"]),
        mesh=mesh,
        in_specs=placed,
        out_specs=P("row", "col"),
        check_vma=False,
    )
```

```python
import functools
import jax
import jax.numpy as jnp
from jax import lax
from jax.experimental import pallas as pl
from jax.experimental.pallas import tpu as pltpu
from jax.sharding import PartitionSpec as P

EXPERTS = 8
CAP = 128
TOK_ROW = 256
MAIN = 320
SLOTS = 3
F32 = jnp.float32
BF16 = jnp.bfloat16
VMEM = 64 * 1024 * 1024


def pack_kernel(chosen, base_ref, ids_ref, tokens_ref, *out_refs):
    tokens = tokens_ref.shape[0]
    numbers = lax.broadcasted_iota(jnp.int32, (EXPERTS, tokens), 0)
    ids = jnp.bitwise_xor(ids_ref[...], base_ref[0])
    hit = (numbers == ids[0:1, :]) | (numbers == ids[1:2, :])
    hits = jnp.where(hit, 1.0, 0.0)
    before = lax.broadcasted_iota(jnp.int32, (tokens, tokens), 0)
    after = lax.broadcasted_iota(jnp.int32, (tokens, tokens), 1)
    upper = jnp.where(before < after, 1.0, 0.0).astype(BF16)
    ranks = jnp.dot(hits.astype(BF16), upper, preferred_element_type=F32)
    ranks = jnp.where(hit, ranks, -1.0)
    slots = lax.broadcasted_iota(jnp.int32, (CAP, tokens), 0).astype(F32)
    for out_ref, experts in zip(out_refs, chosen):
        for index, expert in enumerate(experts):
            picker = jnp.where(slots == ranks[expert : expert + 1, :], 1.0, 0.0).astype(BF16)
            rows = jnp.dot(picker, tokens_ref[...], preferred_element_type=F32)
            out_ref[index] = rows.astype(BF16)


def pack(chosen, base, ids, tokens):
    width = tokens.shape[1]
    vmem = pl.BlockSpec(memory_space=pltpu.VMEM)
    return pl.pallas_call(
        functools.partial(pack_kernel, chosen),
        out_shape=[jax.ShapeDtypeStruct((len(c), CAP, width), BF16) for c in chosen],
        in_specs=[pl.BlockSpec(memory_space=pltpu.SMEM), vmem, vmem],
        out_specs=[vmem] * len(chosen),
        compiler_params=pltpu.CompilerParams(vmem_limit_bytes=VMEM),
        name="pack",
    )(base, ids, tokens)


def stack_kernel(layout, count, *refs):
    sources, index_ref, out_refs = refs[:count], refs[count], refs[-len(layout) :]
    for out_ref, parts in zip(out_refs, layout):
        for index, (source, at) in enumerate(parts):
            out_ref[index] = sources[source][index_ref[at]]


def stack(layout, sources, indices, token=None):
    tokens = () if token is None else (token,)
    vmem = pl.BlockSpec(memory_space=pltpu.VMEM)
    block = sources[0].shape[1:]
    return pl.pallas_call(
        functools.partial(stack_kernel, layout, len(sources)),
        out_shape=[jax.ShapeDtypeStruct((len(parts),) + block, BF16) for parts in layout],
        in_specs=[vmem] * len(sources)
        + [pl.BlockSpec(memory_space=pltpu.SMEM)] * (1 + len(tokens)),
        out_specs=[vmem] * len(layout),
        compiler_params=pltpu.CompilerParams(vmem_limit_bytes=VMEM),
        name="stack",
    )(*sources, indices, *tokens)


def plan_kernel(rows, local, base_ref, *refs):
    ids_refs, busy_ref, flips_ref, starts_ref, spill_ref = refs[:rows], *refs[rows:]
    numbers = lax.broadcasted_iota(jnp.int32, (EXPERTS, TOK_ROW), 0)
    counts = []
    for ids_ref in ids_refs:
        ids = jnp.bitwise_xor(ids_ref[...], base_ref[0])
        hit = (numbers == ids[0:1, :]) | (numbers == ids[1:2, :])
        counts.append(jnp.sum(jnp.where(hit, 1.0, 0.0), axis=1, keepdims=True))
    loads = counts[0]
    for count in counts[1:]:
        loads += count

    def scalar(column, expert):
        return jnp.sum(column[expert : expert + 1, :]).astype(jnp.int32)

    spill = 0
    for k in range(rows):
        first, second = scalar(loads, 2 * k), scalar(loads, 2 * k + 1)
        flip = jnp.where(second > first, 1, 0)
        flips_ref[k] = flip
        spill = jnp.maximum(spill, jnp.minimum(first, second))
        if k == 0:
            small_is_first = flip
            busy_ref[0] = flip
            busy_ref[1] = 1 - flip
    spill_ref[0] = spill
    start = 0
    for k in range(rows):
        starts_ref[k] = start
        first, second = scalar(counts[k], 0), scalar(counts[k], 1)
        start = start + jnp.where(small_is_first == 1, first, second)
    starts_ref[rows] = start


def plan(rows, local, base, all_ids):
    smem = pl.BlockSpec(memory_space=pltpu.SMEM)
    vmem = pl.BlockSpec(memory_space=pltpu.VMEM)
    sizes = [local, rows, rows + 1, 1]
    return pl.pallas_call(
        functools.partial(plan_kernel, rows, local),
        out_shape=[jax.ShapeDtypeStruct((size,), jnp.int32) for size in sizes],
        in_specs=[smem] + [vmem] * rows,
        out_specs=[smem] * 4,
        compiler_params=pltpu.CompilerParams(vmem_limit_bytes=VMEM),
        name="plan",
    )(base, *all_ids)


def tighten_kernel(sizes, count, held, busy_ref, starts_ref, token_ref, *refs):
    sources, out_refs = refs[:count], refs[count + held : count + held + len(sizes)]
    begin = 0
    for out_ref, size in zip(out_refs, sizes):
        slot = lax.broadcasted_iota(jnp.int32, (size, CAP), 0) + begin
        rank = lax.broadcasted_iota(jnp.int32, (size, CAP), 1)
        total = jnp.zeros(out_ref.shape, F32)
        for k, source in enumerate(sources):
            at = rank + starts_ref[k]
            picker = jnp.where((slot == at) & (at < starts_ref[k + 1]), 1.0, 0.0).astype(BF16)
            total += jnp.dot(picker, source[busy_ref[1]], preferred_element_type=F32)
        out_ref[...] = total.astype(BF16)
        begin += size


def tighten(sizes, busy, starts, token, sources, held):
    smem = pl.BlockSpec(memory_space=pltpu.SMEM)
    vmem = pl.BlockSpec(memory_space=pltpu.VMEM)
    anywhere = pl.BlockSpec(memory_space=pl.ANY)
    width, first = sources[0].shape[2], 3 + len(sources)
    out_shape = [jax.ShapeDtypeStruct((size, width), BF16) for size in sizes]
    out_shape += [jax.ShapeDtypeStruct(array.shape, array.dtype) for array in held]
    return pl.pallas_call(
        functools.partial(tighten_kernel, sizes, len(sources), len(held)),
        out_shape=out_shape,
        in_specs=[smem] * 3 + [vmem] * len(sources) + [anywhere] * len(held),
        out_specs=[vmem] * len(sizes) + [anywhere] * len(held),
        input_output_aliases={first + i: len(sizes) + i for i in range(len(held))},
        compiler_params=pltpu.CompilerParams(vmem_limit_bytes=VMEM),
        name="tighten",
    )(busy, starts, token, *sources, *held)


def loosen_kernel(rows, starts_ref, rest_ref, *refs):
    terms, out_refs = refs[:-rows], refs[-rows:]
    total = terms[0][...].astype(F32)
    for term in terms[1:]:
        total += term[...].astype(F32)
    total = total.astype(BF16)
    begin = 0
    outs = [jnp.zeros(out_ref.shape, F32) for out_ref in out_refs]
    for part in (total, rest_ref[...]):
        slot = lax.broadcasted_iota(jnp.int32, (CAP, part.shape[0]), 1) + begin
        rank = lax.broadcasted_iota(jnp.int32, (CAP, part.shape[0]), 0)
        for k in range(rows):
            at = rank + starts_ref[k]
            picker = jnp.where((slot == at) & (at < starts_ref[k + 1]), 1.0, 0.0).astype(BF16)
            outs[k] += jnp.dot(picker, part, preferred_element_type=F32)
        begin += part.shape[0]
    for out_ref, out in zip(out_refs, outs):
        out_ref[...] = out.astype(BF16)


def loosen(rows, starts, rest, terms):
    vmem = pl.BlockSpec(memory_space=pltpu.VMEM)
    block = jax.ShapeDtypeStruct((CAP, rest.shape[1]), BF16)
    return pl.pallas_call(
        functools.partial(loosen_kernel, rows),
        out_shape=[block] * rows,
        in_specs=[pl.BlockSpec(memory_space=pltpu.SMEM)] + [vmem] * (1 + len(terms)),
        out_specs=[vmem] * rows,
        compiler_params=pltpu.CompilerParams(vmem_limit_bytes=VMEM),
        name="loosen",
    )(starts, rest, *terms)


def combine_kernel(experts, count, base_ref, flips_ref, ids_ref, weights_ref, start_ref, *refs):
    slot_refs, out_ref = refs[:-1], refs[-1]
    tokens = start_ref.shape[0]
    ids = jnp.bitwise_xor(ids_ref[...], base_ref[0])
    for k in range(count):
        ids = jnp.where(ids // 2 == k, jnp.bitwise_xor(ids, flips_ref[k]), ids)
    ids = ids.astype(F32)
    filler = jnp.zeros((4, tokens), F32)
    columns = jnp.transpose(jnp.concatenate([ids, weights_ref[...], filler], axis=0))
    lanes = lax.broadcasted_iota(jnp.int32, (tokens, 128), 1).astype(F32)
    first, second = columns[:, 0:1], columns[:, 1:2]
    hits = jnp.where((lanes == first) | (lanes == second), 1.0, 0.0)
    row = lax.broadcasted_iota(jnp.int32, (tokens, tokens), 0)
    column = lax.broadcasted_iota(jnp.int32, (tokens, tokens), 1)
    lower = jnp.where(column < row, 1.0, 0.0).astype(BF16)
    ranks = jnp.dot(lower, hits.astype(BF16), preferred_element_type=F32)
    total = start_ref[...].astype(F32)
    for choice, chosen in enumerate((first, second)):
        rank = jnp.sum(jnp.where(lanes == chosen, ranks, 0.0), axis=1, keepdims=True)
        matches = jnp.where(lanes == rank, 1.0, 0.0)
        picked = jnp.zeros(total.shape, F32)
        for expert, slot_ref in zip(experts, slot_refs):
            picker = jnp.where(chosen == expert, matches, 0.0).astype(BF16)
            picked += jnp.dot(picker, slot_ref[...], preferred_element_type=F32)
        total += picked * columns[:, 2 + choice : 3 + choice]
    out_ref[...] = total.astype(out_ref.dtype)


def combine(experts, base, flips, ids, gate_weights, start, slots, kind):
    count = flips.shape[0] if EXPERTS == 2 * flips.shape[0] else 0
    vmem = pl.BlockSpec(memory_space=pltpu.VMEM)
    return pl.pallas_call(
        functools.partial(combine_kernel, experts, count),
        out_shape=jax.ShapeDtypeStruct(start.shape, kind),
        in_specs=[pl.BlockSpec(memory_space=pltpu.SMEM)] * 2 + [vmem] * (3 + len(slots)),
        out_specs=vmem,
        compiler_params=pltpu.CompilerParams(vmem_limit_bytes=VMEM),
        name="combine",
    )(base, flips, ids, gate_weights, start, *slots)


def up_kernel(number, segments, cols, places, place_ref, experts_ref, gain_ref, *refs):
    count = len(segments) * cols
    expert = experts_ref[number]
    pieces = refs[:count]
    w_gate, w_up, w_down = refs[count : count + 3]
    (send_out, early_out, hidden_out, done_out, raw, scaled, ups, downs, hidden, staged, total, squares) = refs[-18:-6]
    x_sem, gate_sem, up_sem, down_sem, out_sem, hidden_sem = refs[-6:]
    slots, features = ups.shape[0], ups.shape[1]
    tile, units, width = ups.shape[2] // 2, hidden.shape[1], raw.shape[2]
    tiles, half = units // tile, cols // 2
    place = place_ref[0]
    done_out[0] = place

    def up_copies(index):
        slot = lax.rem(index, slots)
        columns = pl.ds(pl.multiple_of(index * tile, tile), tile)
        return (
            pltpu.make_async_copy(
                w_gate.at[expert, :, columns], ups.at[slot, :, pl.ds(0, tile)], gate_sem.at[slot]
            ),
            pltpu.make_async_copy(
                w_up.at[expert, :, columns], ups.at[slot, :, pl.ds(tile, tile)], up_sem.at[slot]
            ),
        )

    def down_copy(index):
        core, at = (1, index) if index < half else (0, index - half)
        return down_piece(expert, w_down, downs, down_sem, place, index, at, core)

    def piece_copies(relative):
        copies = []
        start = 0
        for segment, rows in enumerate(segments):
            number = segment * cols + relative
            piece, at = pieces[number], places[number]
            if at is None:
                source = piece.at[jnp.bitwise_xor(place, relative)]
            else:
                source = piece.at[at]
            target = raw.at[relative, pl.ds(start, rows), :]
            copies.append(pltpu.make_async_copy(source, target, x_sem.at[number]))
            start += rows
        return copies

    for relative in range(cols):
        for copy in piece_copies(relative):
            copy.start()
    for copy in up_copies(0):
        copy.start()
    for relative in range(cols):
        for copy in piece_copies(relative):
            copy.wait()
        values = raw[relative].astype(F32)
        square = values * values
        part = square[:, 0:128]
        for lane in range(128, width, 128):
            part += square[:, lane : lane + 128]
        if relative == 0:
            squares[...] = part
        else:
            squares[...] += part
    for index in range(1, slots):
        for copy in up_copies(index):
            copy.start()
    mean = jnp.sum(squares[...], axis=1, keepdims=True) * (1.0 / features)
    inverse = lax.rsqrt(mean + 1e-05)
    for copy in up_copies(0):
        copy.wait()
    for relative in range(cols):
        owner = jnp.bitwise_xor(place, relative)
        at = pl.ds(pl.multiple_of(owner * width, width), width)
        share = (raw[relative].astype(F32) * inverse * gain_ref[owner]).astype(BF16)
        scaled[:, at] = share
        product = jnp.dot(share, ups[0, at, :], preferred_element_type=F32)
        if relative == 0:
            total[...] = product
        else:
            total[...] += product

    def activate(both, columns):
        gate, up = both[:, :tile], both[:, tile:]
        hidden[:, columns] = (gate / (1.0 + jnp.exp(-gate)) * up).astype(BF16)

    activate(total[...], pl.ds(0, tile))

    @pl.loop(1, tiles)
    def _(index):
        for copy in up_copies(index):
            copy.wait()

        @pl.when(index + slots - 1 < tiles)
        def _():
            for copy in up_copies(index + slots - 1):
                copy.start()

        for step in range(half + half // 2):

            @pl.when(index == tiles - slots + 1 + step * (slots - 1) // (half + half // 2))
            def _():
                down_copy(step).start()

        both = jnp.dot(scaled[...], ups[lax.rem(index, slots)], preferred_element_type=F32)
        activate(both, pl.ds(pl.multiple_of(index * tile, tile), tile))

    hidden_copy = pltpu.make_async_copy(hidden, hidden_out, hidden_sem)
    hidden_copy.start()
    targets = [send_out.at[index] for index in range(half)]
    targets += [early_out.at[index] for index in range(half // 2)]
    finish_down(targets, hidden, downs, staged, down_copy, out_sem)
    hidden_copy.wait()


def down_piece(expert, w_down, downs, down_sem, place, slot, index, core):
    width = downs.shape[2] // 2
    owner = jnp.bitwise_xor(place, 2 * index + core)
    return pltpu.make_async_copy(
        w_down.at[expert, :, pl.ds(pl.multiple_of(owner * width, width), width)],
        downs.at[slot // 2, :, pl.ds(slot % 2 * width, width)],
        down_sem.at[slot],
    )


def finish_down(targets, hidden, downs, staged, down_copy, out_sem):
    outs = []
    width = downs.shape[2] // 2
    for index in range(0, len(targets), 2):
        down_copy(index).wait()
        down_copy(index + 1).wait()
        both = jnp.dot(hidden[...], downs[index // 2], preferred_element_type=F32).astype(BF16)
        for at in (index, index + 1):
            start = (at - index) * width
            staged[at] = both[:, start : start + width]
            outs.append(pltpu.make_async_copy(staged.at[at], targets[at], out_sem.at[at]))
            outs[-1].start()
    for out in outs:
        out.wait()


def down_kernel(number, count, place_ref, experts_ref, hidden_ref, w_down, *refs):
    terms = refs[:count]
    expert = experts_ref[number]
    hidden, downs, staged, down_sem, out_sem, hidden_sem = refs[-6:]
    late = staged.shape[0]

    def down_copy(index):
        return down_piece(expert, w_down, downs, down_sem, place_ref[0], index, late + index, 0)

    hidden_copy = pltpu.make_async_copy(hidden_ref, hidden, hidden_sem)
    hidden_copy.start()
    if count:
        late_out, low_out, high_out, held, summed, term_sem, sum_sem = refs[-13:-6]
        copies = [
            pltpu.make_async_copy(terms[index], held.at[index], term_sem.at[index])
            for index in range(count)
        ]
        for copy in copies:
            copy.start()
    else:
        late_out = refs[-7]
    for index in range(late):
        down_copy(index).start()
    outs = []
    if count:
        for copy in copies:
            copy.wait()
        total = held[0].astype(F32)
        for index in range(1, count):
            total += held[index].astype(F32)
        summed[...] = total.astype(BF16)
        for index, out_ref in enumerate((low_out, high_out)):
            rows = pl.ds(index * CAP, CAP)
            outs.append(pltpu.make_async_copy(summed.at[rows], out_ref, sum_sem.at[index]))
            outs[-1].start()
    hidden_copy.wait()
    targets = [late_out.at[index] for index in range(late)]
    finish_down(targets, hidden, downs, staged, down_copy, out_sem)
    for out in outs:
        out.wait()


def expand(number, experts, pieces, place, norm_gain, w_gate, w_up, w_down, after=()):
    cols = len(pieces[0])
    segments = [run[0][0].shape[-2] for run in pieces]
    features, units = w_gate.shape[1], w_gate.shape[2]
    width, rows, half = features // cols, sum(segments), cols // 2
    tile = 256 if units % 256 == 0 else 128
    anywhere = pl.BlockSpec(memory_space=pl.ANY)
    flat = [array for block in pieces for array, _ in block]
    places = [index for block in pieces for _, index in block]
    downs = half + half // 2
    weights = 2 * features * units + downs * units * width
    return pl.pallas_call(
        functools.partial(up_kernel, number, segments, cols, places),
        out_shape=[
            jax.ShapeDtypeStruct((half, rows, width), BF16),
            jax.ShapeDtypeStruct((half // 2, rows, width), BF16),
            jax.ShapeDtypeStruct((rows, units), BF16),
            jax.ShapeDtypeStruct((1,), jnp.int32),
        ],
        in_specs=[
            pl.BlockSpec(memory_space=pltpu.SMEM),
            pl.BlockSpec(memory_space=pltpu.SMEM),
            pl.BlockSpec(memory_space=pltpu.VMEM),
        ]
        + [anywhere] * (len(flat) + 3 + len(after)),
        out_specs=[anywhere, anywhere, anywhere, pl.BlockSpec(memory_space=pltpu.SMEM)],
        scratch_shapes=[
            pltpu.VMEM((cols, rows, width), BF16),
            pltpu.VMEM((rows, features), BF16),
            pltpu.VMEM((SLOTS, features, 2 * tile), BF16),
            pltpu.VMEM((downs // 2, units, 2 * width), BF16),
            pltpu.VMEM((rows, units), BF16),
            pltpu.VMEM((downs, rows, width), BF16),
            pltpu.VMEM((rows, 2 * tile), F32),
            pltpu.VMEM((rows, 128), F32),
            pltpu.SemaphoreType.DMA((len(flat),)),
            pltpu.SemaphoreType.DMA((SLOTS,)),
            pltpu.SemaphoreType.DMA((SLOTS,)),
            pltpu.SemaphoreType.DMA((downs,)),
            pltpu.SemaphoreType.DMA((downs,)),
            pltpu.SemaphoreType.DMA,
        ],
        compiler_params=pltpu.CompilerParams(vmem_limit_bytes=VMEM),
        cost_estimate=pl.CostEstimate(
            flops=2 * rows * weights, bytes_accessed=2 * weights, transcendentals=rows * units
        ),
        name="expand",
    )(place, experts, norm_gain.reshape(cols, 1, width), *flat, w_gate, w_up, w_down, *after)


def contract(number, experts, hidden, cols, place, w_down, terms=(), after=()):
    rows, units = hidden.shape
    width, late, count = w_down.shape[2] // cols, cols // 4, len(terms)
    anywhere = pl.BlockSpec(memory_space=pl.ANY)
    weights = units * width * late
    block = jax.ShapeDtypeStruct((CAP, width), BF16)
    side = [
        pltpu.VMEM((count, 2 * CAP, width), BF16),
        pltpu.VMEM((2 * CAP, width), BF16),
        pltpu.SemaphoreType.DMA((count,)),
        pltpu.SemaphoreType.DMA((2,)),
    ]
    out_shape = [jax.ShapeDtypeStruct((late, rows, width), BF16)] + [block, block] * bool(count)
    return pl.pallas_call(
        functools.partial(down_kernel, number, count),
        out_shape=out_shape,
        in_specs=[pl.BlockSpec(memory_space=pltpu.SMEM)] * 2 + [anywhere] * (2 + count + len(after)),
        out_specs=[anywhere] * len(out_shape),
        scratch_shapes=side * bool(count)
        + [
            pltpu.VMEM((rows, units), BF16),
            pltpu.VMEM((late // 2, units, 2 * width), BF16),
            pltpu.VMEM((late, rows, width), BF16),
            pltpu.SemaphoreType.DMA((late,)),
            pltpu.SemaphoreType.DMA((late,)),
            pltpu.SemaphoreType.DMA,
        ],
        compiler_params=pltpu.CompilerParams(vmem_limit_bytes=VMEM),
        cost_estimate=pl.CostEstimate(
            flops=128 * rows * weights, bytes_accessed=128 * weights, transcendentals=0
        ),
        name="contract",
    )(place, experts, hidden, w_down, *terms, *after)


def pair_kernel(early_ref, late_ref, other_ref, *refs):
    half = other_ref.shape[0]
    out_refs = refs[:half]
    mine, other, staged, mine_sem, other_sem, out_sem = refs[half:]
    copies = []
    for index in range(half):
        source, at = (early_ref, index) if index < half // 2 else (late_ref, index - half // 2)
        copies.append(
            (
                pltpu.make_async_copy(source.at[at], mine.at[index], mine_sem.at[index]),
                pltpu.make_async_copy(other_ref.at[index], other.at[index], other_sem.at[index]),
            )
        )
    for ours, theirs in copies:
        ours.start()
        theirs.start()
    outs = []
    for index in range(half):
        for copy in copies[index]:
            copy.wait()
        both = mine[index].astype(F32) + other[index].astype(F32)
        staged[index] = both.astype(BF16)
        outs.append(pltpu.make_async_copy(staged.at[index], out_refs[index], out_sem.at[index]))
        outs[-1].start()
    for out in outs:
        out.wait()


def pair_sums(early, late, other):
    half, block = other.shape[0], other.shape[1:]
    anywhere = pl.BlockSpec(memory_space=pl.ANY)
    return pl.pallas_call(
        pair_kernel,
        out_shape=[jax.ShapeDtypeStruct(block, BF16)] * half,
        in_specs=[anywhere] * 3,
        out_specs=[anywhere] * half,
        scratch_shapes=[pltpu.VMEM(other.shape, BF16)] * 3 + [pltpu.SemaphoreType.DMA((half,))] * 3,
        compiler_params=pltpu.CompilerParams(vmem_limit_bytes=VMEM),
        name="pair_sums",
    )(early, late, other)


def add_kernel(count, *refs):
    terms, out_refs = refs[:count], refs[-2:]
    total = terms[0][...].astype(F32)
    for term in terms[1:]:
        total += term[...].astype(F32)
    for index, out_ref in enumerate(out_refs):
        out_ref[...] = total[index * CAP : (index + 1) * CAP].astype(BF16)


def add(terms):
    vmem = pl.BlockSpec(memory_space=pltpu.VMEM)
    block = jax.ShapeDtypeStruct((CAP, terms[0].shape[1]), BF16)
    return pl.pallas_call(
        functools.partial(add_kernel, len(terms)),
        out_shape=[block, block],
        in_specs=[vmem] * len(terms),
        out_specs=[vmem, vmem],
        compiler_params=pltpu.CompilerParams(vmem_limit_bytes=VMEM),
        name="add",
    )(*terms)


def movers(rows, cols):
    def along_row(value, relative):
        if relative == 0:
            return value
        return lax.ppermute(value, "row", [(i, i ^ relative) for i in range(rows)])

    def along_col(value, relative):
        if relative == 0:
            return value
        return lax.ppermute(value, "col", [(i, i ^ relative) for i in range(cols)])

    def gather(shares):
        return [along_col(shares, q) for q in range(0, cols, 2)]

    def complete(same_core):
        other_core = [along_col(piece, 1) for piece in same_core]
        return [piece for pair in zip(same_core, other_core) for piece in pair]

    return along_row, along_col, gather, complete


def blocks_of(pieces):
    return [[(p, block) for p in pieces] for block in range(2)]


def body_one(rows, cols, tokens, norm_gain, expert_ids, gate_weights, w_gate, w_up, w_down):
    along_row, along_col, gather, complete = movers(rows, cols)
    row, place = lax.axis_index("row"), lax.axis_index("col").reshape(1)
    base = row.reshape(1)
    ids, token_weights = expert_ids.T, gate_weights.T
    experts = jnp.zeros((1,), jnp.int32)
    packed = pack([[k] for k in range(rows)], base, ids, tokens)
    arrived = [along_row(packed[k], k) for k in range(rows)]
    returned, pairs = [], []
    for first in range(0, rows, 2):
        shares = stack([[(0, 0), (1, 0)]], arrived[first : first + 2], experts)[0]
        pieces = blocks_of(complete(gather(shares)))
        send, early, hidden, _ = expand(
            0, experts, pieces, place, norm_gain, w_gate, w_up, w_down, after=pairs
        )
        got = along_col(send, 1)
        late = contract(0, experts, hidden, cols, place, w_down)[0]
        pairs = pair_sums(early, late, got)
        totals = add([along_col(share, 2 * q) for q, share in enumerate(pairs)])
        returned += [along_row(total, first + block) for block, total in enumerate(totals)]
    return combine(range(rows), base, base, ids, token_weights, tokens, returned, BF16)


def body_two(rows, cols, tokens, norm_gain, expert_ids, gate_weights, w_gate, w_up, w_down):
    along_row, along_col, gather, complete = movers(rows, cols)
    row, place = lax.axis_index("row"), lax.axis_index("col").reshape(1)
    base = (row * 2).reshape(1)
    ids, token_weights = expert_ids.T, gate_weights.T
    packed = pack([[2 * k, 2 * k + 1] for k in range(rows)], base, ids, tokens)
    arrived = [along_row(packed[k], k) for k in range(rows)]
    busy, flips, starts, spill = plan(rows, 2, base, [along_row(ids, k) for k in range(rows)])
    weights = (place, norm_gain, w_gate, w_up, w_down)

    def reduce(number, send, early, hidden, terms, after):
        got = along_col(send, 1)
        late, *totals = contract(
            number, busy, hidden, cols, place, w_down, terms=terms, after=after
        )
        pairs = pair_sums(early, late, got)
        return pairs, [along_col(share, 2 * q) for q, share in enumerate(pairs)], totals

    shares = [stack([[(0, 0), (1, 0)]], arrived[k : k + 2], busy)[0] for k in range(0, rows, 2)]
    parts = [gather(share) for share in shares]
    pieces = blocks_of(complete(parts[0]))
    send, early, hidden, done = expand(0, busy, pieces, *weights, after=shares[1:])
    sizes = (MAIN, rows * CAP - MAIN)
    main, rest, *parts[1] = tighten(sizes, busy, starts, done, arrived, parts[1])
    everyone = lax.all_gather(main, "col", axis=0)
    pairs, terms, _ = reduce(0, send, early, hidden, (), [main])
    returned, home = {}, []
    for chunk in range(1, rows // 2 + 1):
        if chunk < rows // 2:
            pieces, number = blocks_of(complete(parts[chunk])), 0
        else:
            pieces, number = [[(everyone, None)] * cols], 1
        send, early, hidden, _ = expand(number, busy, pieces, *weights, after=pairs)
        pairs, next_terms, totals = reduce(number, send, early, hidden, terms, home)
        home = []
        for k, total in zip((2 * chunk - 2, 2 * chunk - 1), totals):
            returned[2 * k] = along_row(total, k)
            home.append(returned[2 * k])
        terms = next_terms

    def extra(last):
        pieces = [[(piece, 0) for piece in complete(gather(rest.reshape(1, *rest.shape)))]]
        send, early, hidden, _ = expand(1, busy, pieces, *weights, after=[last])
        _, terms, _ = reduce(1, send, early, hidden, (), ())
        total = terms[0].astype(F32)
        for term in terms[1:]:
            total += term.astype(F32)
        return total.astype(BF16)

    more = lax.cond(spill[0] > MAIN, extra, lambda _: jnp.zeros(rest.shape, BF16), pairs[0])
    numbers = sorted(returned)
    slots = [returned[number] for number in numbers]
    partial = combine(numbers, base, flips, ids, token_weights, tokens, slots, F32)
    totals = loosen(rows, starts, more, terms)
    slots = [along_row(total, k) for k, total in enumerate(totals)]
    numbers = [2 * k + 1 for k in range(rows)]
    return combine(numbers, base, flips, ids, token_weights, partial, slots, BF16)


def solution(mesh):
    placed = (
        P("row", "col"),
        P(),
        P("row", None),
        P("row", None),
        P("row", None, "col"),
        P("row", None, "col"),
        P("row", "col", None),
    )
    body = body_two if EXPERTS == 2 * mesh.shape["row"] else body_one
    return jax.shard_map(
        functools.partial(body, mesh.shape["row"], mesh.shape["col"]),
        mesh=mesh,
        in_specs=placed,
        out_specs=P("row", "col"),
        check_vma=False,
    )
```

```python
import functools
import jax
import jax.numpy as jnp
from jax import lax
from jax.experimental import pallas as pl
from jax.experimental.pallas import tpu as pltpu
from jax.sharding import PartitionSpec as P

EXPERTS = 8
CAP = 128
TOK_ROW = 256
MAIN = 336
SLOTS = 4
F32 = jnp.float32
BF16 = jnp.bfloat16
VMEM = 64 * 1024 * 1024


def pack_kernel(chosen, base_ref, ids_ref, tokens_ref, *out_refs):
    tokens = tokens_ref.shape[0]
    numbers = lax.broadcasted_iota(jnp.int32, (EXPERTS, tokens), 0)
    ids = jnp.bitwise_xor(ids_ref[...], base_ref[0])
    hit = (numbers == ids[0:1, :]) | (numbers == ids[1:2, :])
    hits = jnp.where(hit, 1.0, 0.0)
    before = lax.broadcasted_iota(jnp.int32, (tokens, tokens), 0)
    after = lax.broadcasted_iota(jnp.int32, (tokens, tokens), 1)
    upper = jnp.where(before < after, 1.0, 0.0).astype(BF16)
    ranks = jnp.dot(hits.astype(BF16), upper, preferred_element_type=F32)
    ranks = jnp.where(hit, ranks, -1.0)
    slots = lax.broadcasted_iota(jnp.int32, (CAP, tokens), 0).astype(F32)
    for out_ref, experts in zip(out_refs, chosen):
        for index, expert in enumerate(experts):
            picker = jnp.where(slots == ranks[expert : expert + 1, :], 1.0, 0.0).astype(BF16)
            rows = jnp.dot(picker, tokens_ref[...], preferred_element_type=F32)
            out_ref[index] = rows.astype(BF16)


def pack(chosen, base, ids, tokens):
    width = tokens.shape[1]
    vmem = pl.BlockSpec(memory_space=pltpu.VMEM)
    return pl.pallas_call(
        functools.partial(pack_kernel, chosen),
        out_shape=[jax.ShapeDtypeStruct((len(c), CAP, width), BF16) for c in chosen],
        in_specs=[pl.BlockSpec(memory_space=pltpu.SMEM), vmem, vmem],
        out_specs=[vmem] * len(chosen),
        compiler_params=pltpu.CompilerParams(vmem_limit_bytes=VMEM),
        name="pack",
    )(base, ids, tokens)


def stack_kernel(layout, count, *refs):
    sources, index_ref, out_refs = refs[:count], refs[count], refs[-len(layout) :]
    for out_ref, parts in zip(out_refs, layout):
        for index, (source, at) in enumerate(parts):
            out_ref[index] = sources[source][index_ref[at]]


def stack(layout, sources, indices):
    vmem = pl.BlockSpec(memory_space=pltpu.VMEM)
    block = sources[0].shape[1:]
    return pl.pallas_call(
        functools.partial(stack_kernel, layout, len(sources)),
        out_shape=[jax.ShapeDtypeStruct((len(parts),) + block, BF16) for parts in layout],
        in_specs=[vmem] * len(sources) + [pl.BlockSpec(memory_space=pltpu.SMEM)],
        out_specs=[vmem] * len(layout),
        compiler_params=pltpu.CompilerParams(vmem_limit_bytes=VMEM),
        name="stack",
    )(*sources, indices)


def plan_kernel(rows, local, base_ref, *refs):
    ids_refs, sources = refs[:rows], refs[rows : rows + 2]
    busy_ref, flips_ref, starts_ref, spill_ref, shares_ref = refs[rows + 2 :]
    numbers = lax.broadcasted_iota(jnp.int32, (EXPERTS, TOK_ROW), 0)
    counts = []
    for ids_ref in ids_refs:
        ids = jnp.bitwise_xor(ids_ref[...], base_ref[0])
        hit = (numbers == ids[0:1, :]) | (numbers == ids[1:2, :])
        counts.append(jnp.sum(jnp.where(hit, 1.0, 0.0), axis=1, keepdims=True))
    loads = counts[0]
    for count in counts[1:]:
        loads += count

    def scalar(column, expert):
        return jnp.sum(column[expert : expert + 1, :]).astype(jnp.int32)

    spill = 0
    for k in range(rows):
        first, second = scalar(loads, 2 * k), scalar(loads, 2 * k + 1)
        flip = jnp.where(second > first, 1, 0)
        flips_ref[k] = flip
        spill = jnp.maximum(spill, jnp.minimum(first, second))
        if k == 0:
            small_is_first = flip
            for index, source in enumerate(sources):
                shares_ref[index * CAP : (index + 1) * CAP] = source[flip]
            busy_ref[0] = flip
            busy_ref[1] = 1 - flip
    spill_ref[0] = spill
    start = 0
    for k in range(rows):
        starts_ref[k] = start
        first, second = scalar(counts[k], 0), scalar(counts[k], 1)
        start = start + jnp.where(small_is_first == 1, first, second)
    starts_ref[rows] = start


def plan(rows, local, base, all_ids, sources):
    smem = pl.BlockSpec(memory_space=pltpu.SMEM)
    vmem = pl.BlockSpec(memory_space=pltpu.VMEM)
    sizes = [local, rows, rows + 1, 1]
    return pl.pallas_call(
        functools.partial(plan_kernel, rows, local),
        out_shape=[jax.ShapeDtypeStruct((size,), jnp.int32) for size in sizes]
        + [jax.ShapeDtypeStruct((2 * CAP, sources[0].shape[2]), BF16)],
        in_specs=[smem] + [vmem] * (rows + 2),
        out_specs=[smem] * 4 + [vmem],
        compiler_params=pltpu.CompilerParams(vmem_limit_bytes=VMEM),
        name="plan",
    )(base, *all_ids, *sources)


def join_kernel(busy_ref, starts_ref, *refs):
    sources, joined_ref, rest_ref = refs[:-2], refs[-2], refs[-1]
    far = (len(sources) - 2) * CAP
    for index, source in enumerate(sources[2:]):
        joined_ref[index * CAP : (index + 1) * CAP] = source[busy_ref[0]]
    for out_ref, at_row, size, begin in (
        (joined_ref, far, MAIN, 0),
        (rest_ref, 0, rest_ref.shape[0], MAIN),
    ):
        slot = lax.broadcasted_iota(jnp.int32, (size, CAP), 0) + begin
        rank = lax.broadcasted_iota(jnp.int32, (size, CAP), 1)
        total = jnp.zeros((size, out_ref.shape[1]), F32)
        for k, source in enumerate(sources):
            at = rank + starts_ref[k]
            picker = jnp.where((slot == at) & (at < starts_ref[k + 1]), 1.0, 0.0).astype(BF16)
            total += jnp.dot(picker, source[busy_ref[1]], preferred_element_type=F32)
        out_ref[at_row : at_row + size] = total.astype(BF16)


def join(busy, starts, sources):
    smem = pl.BlockSpec(memory_space=pltpu.SMEM)
    vmem = pl.BlockSpec(memory_space=pltpu.VMEM)
    rows, width = len(sources), sources[0].shape[2]
    sizes = [(rows - 2) * CAP + MAIN, rows * CAP - MAIN]
    return pl.pallas_call(
        join_kernel,
        out_shape=[jax.ShapeDtypeStruct((size, width), BF16) for size in sizes],
        in_specs=[smem] * 2 + [vmem] * rows,
        out_specs=[vmem] * 2,
        compiler_params=pltpu.CompilerParams(vmem_limit_bytes=VMEM),
        name="join",
    )(busy, starts, *sources)


def loosen_kernel(rows, starts_ref, spill_ref, rest_ref, *refs):
    terms, out_refs = refs[:-rows], refs[-rows:]
    total = terms[0][...].astype(F32)
    for term in terms[1:]:
        total += term[...].astype(F32)
    total = total.astype(BF16)
    main = total.shape[0]

    def place_rows(part, begin):
        slot = lax.broadcasted_iota(jnp.int32, (CAP, part.shape[0]), 1) + begin
        rank = lax.broadcasted_iota(jnp.int32, (CAP, part.shape[0]), 0)
        for k in range(rows):
            at = rank + starts_ref[k]
            picker = jnp.where((slot == at) & (at < starts_ref[k + 1]), 1.0, 0.0).astype(BF16)
            yield jnp.dot(picker, part, preferred_element_type=F32).astype(BF16)

    for out_ref, out in zip(out_refs, place_rows(total, 0)):
        out_ref[...] = out

    @pl.when(spill_ref[0] > main)
    def _():
        for out_ref, out in zip(out_refs, place_rows(rest_ref[...], main)):
            out_ref[...] += out


def loosen(rows, starts, spill, rest, terms):
    vmem = pl.BlockSpec(memory_space=pltpu.VMEM)
    block = jax.ShapeDtypeStruct((CAP, rest.shape[1]), BF16)
    return pl.pallas_call(
        functools.partial(loosen_kernel, rows),
        out_shape=[block] * rows,
        in_specs=[pl.BlockSpec(memory_space=pltpu.SMEM)] * 2 + [vmem] * (1 + len(terms)),
        out_specs=[vmem] * rows,
        compiler_params=pltpu.CompilerParams(vmem_limit_bytes=VMEM),
        name="loosen",
    )(starts, spill, rest, *terms)


def combine_kernel(experts, later, count, base_ref, flips_ref, ids_ref, weights_ref, start_ref, *refs):
    slot_refs, out_ref, later_refs = refs[: len(experts)], refs[len(experts)], refs[len(experts) + 1 :]
    tokens = start_ref.shape[0]
    ids = jnp.bitwise_xor(ids_ref[...], base_ref[0])
    for k in range(count):
        ids = jnp.where(ids // 2 == k, jnp.bitwise_xor(ids, flips_ref[k]), ids)
    ids = ids.astype(F32)
    filler = jnp.zeros((4, tokens), F32)
    columns = jnp.transpose(jnp.concatenate([ids, weights_ref[...], filler], axis=0))
    lanes = lax.broadcasted_iota(jnp.int32, (tokens, 128), 1).astype(F32)
    first, second = columns[:, 0:1], columns[:, 1:2]
    hits = jnp.where((lanes == first) | (lanes == second), 1.0, 0.0)
    row = lax.broadcasted_iota(jnp.int32, (tokens, tokens), 0)
    column = lax.broadcasted_iota(jnp.int32, (tokens, tokens), 1)
    lower = jnp.where(column < row, 1.0, 0.0).astype(BF16)
    ranks = jnp.dot(lower, hits.astype(BF16), preferred_element_type=F32)
    total = start_ref[...].astype(F32)
    for choice, chosen in enumerate((first, second)):
        rank = jnp.sum(jnp.where(lanes == chosen, ranks, 0.0), axis=1, keepdims=True)
        matches = jnp.where(lanes == rank, 1.0, 0.0)
        picked = jnp.zeros(total.shape, F32)
        for expert, slot_ref in zip(experts, slot_refs):
            picker = jnp.where(chosen == expert, matches, 0.0).astype(BF16)
            picked += jnp.dot(picker, slot_ref[...], preferred_element_type=F32)
        total += picked * columns[:, 2 + choice : 3 + choice]
        for index, expert in enumerate(later):
            picker = jnp.where(chosen == expert, matches, 0.0).astype(BF16)
            later_refs[choice][:, index * CAP : (index + 1) * CAP] = picker
    out_ref[...] = total.astype(out_ref.dtype)
    if later:
        later_refs[2][...] = columns


def combine(experts, later, base, flips, ids, gate_weights, start, slots, kind):
    tokens = start.shape[0]
    pickers = [jax.ShapeDtypeStruct((tokens, CAP * len(later)), BF16)] * 2
    extra = pickers + [jax.ShapeDtypeStruct((tokens, 8), F32)] if later else []
    count = flips.shape[0] if EXPERTS == 2 * flips.shape[0] else 0
    vmem = pl.BlockSpec(memory_space=pltpu.VMEM)
    return pl.pallas_call(
        functools.partial(combine_kernel, experts, later, count),
        out_shape=[jax.ShapeDtypeStruct(start.shape, kind)] + extra,
        in_specs=[pl.BlockSpec(memory_space=pltpu.SMEM)] * 2 + [vmem] * (3 + len(slots)),
        out_specs=[vmem] * (1 + len(extra)),
        compiler_params=pltpu.CompilerParams(vmem_limit_bytes=VMEM),
        name="combine",
    )(base, flips, ids, gate_weights, start, *slots)


def finish_kernel(start_ref, first_ref, second_ref, columns_ref, *refs):
    slot_refs, out_ref = refs[:-1], refs[-1]
    total = start_ref[...]
    for choice, picker_ref in enumerate((first_ref, second_ref)):
        picked = jnp.zeros(total.shape, F32)
        for index, slot_ref in enumerate(slot_refs):
            picker = picker_ref[:, index * CAP : (index + 1) * CAP]
            picked += jnp.dot(picker, slot_ref[...], preferred_element_type=F32)
        total += picked * columns_ref[:, 2 + choice : 3 + choice]
    out_ref[...] = total.astype(out_ref.dtype)


def finish(start, pickers, slots):
    vmem = pl.BlockSpec(memory_space=pltpu.VMEM)
    return pl.pallas_call(
        finish_kernel,
        out_shape=jax.ShapeDtypeStruct(start.shape, BF16),
        in_specs=[vmem] * (1 + len(pickers) + len(slots)),
        out_specs=vmem,
        compiler_params=pltpu.CompilerParams(vmem_limit_bytes=VMEM),
        name="finish",
    )(start, *pickers, *slots)


def up_kernel(number, start, cols, place_ref, experts_ref, gain_ref, *refs):
    count = cols
    expert = experts_ref[number]
    pieces = refs[:count]
    w_gate, w_up, w_down = refs[count : count + 3]
    (send_out, early_out, hidden_out, raw, scaled, ups, downs, hidden, staged, total, squares) = refs[-17:-6]
    x_sem, gate_sem, up_sem, down_sem, out_sem, hidden_sem = refs[-6:]
    slots, features = ups.shape[0], ups.shape[1]
    tile, units, width = ups.shape[2] // 2, hidden.shape[1], raw.shape[2]
    tiles, half = units // tile, cols // 2
    place = place_ref[0]

    def up_copies(index):
        slot = lax.rem(index, slots)
        columns = pl.ds(pl.multiple_of(index * tile, tile), tile)
        return (
            pltpu.make_async_copy(
                w_gate.at[expert, :, columns], ups.at[slot, :, pl.ds(0, tile)], gate_sem.at[slot]
            ),
            pltpu.make_async_copy(
                w_up.at[expert, :, columns], ups.at[slot, :, pl.ds(tile, tile)], up_sem.at[slot]
            ),
        )

    def down_copy(index):
        core, at = (1, index) if index < half else (0, index - half)
        return down_piece(expert, w_down, downs, down_sem, place, index, at, core)

    def piece_copy(relative):
        rows = pl.ds(start, raw.shape[1])
        return pltpu.make_async_copy(
            pieces[relative].at[rows], raw.at[relative], x_sem.at[relative]
        )

    for relative in range(cols):
        piece_copy(relative).start()
    for copy in up_copies(0):
        copy.start()
    for relative in range(cols):
        piece_copy(relative).wait()
        values = raw[relative].astype(F32)
        square = values * values
        part = square[:, 0:128]
        for lane in range(128, width, 128):
            part += square[:, lane : lane + 128]
        if relative == 0:
            squares[...] = part
        else:
            squares[...] += part
    for index in range(1, slots):
        for copy in up_copies(index):
            copy.start()
    mean = jnp.sum(squares[...], axis=1, keepdims=True) * (1.0 / features)
    inverse = lax.rsqrt(mean + 1e-05)
    for copy in up_copies(0):
        copy.wait()
    for relative in range(cols):
        owner = jnp.bitwise_xor(place, relative)
        at = pl.ds(pl.multiple_of(owner * width, width), width)
        share = (raw[relative].astype(F32) * inverse * gain_ref[owner]).astype(BF16)
        scaled[:, at] = share
        product = jnp.dot(share, ups[0, at, :], preferred_element_type=F32)
        if relative == 0:
            total[...] = product
        else:
            total[...] += product

    def activate(both, columns):
        gate, up = both[:, :tile], both[:, tile:]
        hidden[:, columns] = (gate / (1.0 + jnp.exp(-gate)) * up).astype(BF16)

    activate(total[...], pl.ds(0, tile))

    @pl.loop(1, tiles)
    def _(index):
        for copy in up_copies(index):
            copy.wait()

        @pl.when(index + slots - 1 < tiles)
        def _():
            for copy in up_copies(index + slots - 1):
                copy.start()

        for step in range(half + half // 2):

            @pl.when(index == tiles - slots + 1 + step * (slots - 1) // (half + half // 2))
            def _():
                down_copy(step).start()

        both = jnp.dot(scaled[...], ups[lax.rem(index, slots)], preferred_element_type=F32)
        activate(both, pl.ds(pl.multiple_of(index * tile, tile), tile))

    hidden_copy = pltpu.make_async_copy(hidden, hidden_out, hidden_sem)
    hidden_copy.start()
    targets = [send_out.at[index] for index in range(half)]
    targets += [early_out.at[index] for index in range(half // 2)]
    finish_down(targets, hidden, downs, staged, down_copy, out_sem)
    hidden_copy.wait()


def down_piece(expert, w_down, downs, down_sem, place, slot, index, core):
    width = downs.shape[2] // 2
    owner = jnp.bitwise_xor(place, 2 * index + core)
    return pltpu.make_async_copy(
        w_down.at[expert, :, pl.ds(pl.multiple_of(owner * width, width), width)],
        downs.at[slot // 2, :, pl.ds(slot % 2 * width, width)],
        down_sem.at[slot],
    )


def finish_down(targets, hidden, downs, staged, down_copy, out_sem):
    outs = []
    width = downs.shape[2] // 2
    for index in range(0, len(targets), 2):
        down_copy(index).wait()
        down_copy(index + 1).wait()
        both = jnp.dot(hidden[...], downs[index // 2], preferred_element_type=F32).astype(BF16)
        for at in (index, index + 1):
            start = (at - index) * width
            staged[at] = both[:, start : start + width]
            outs.append(pltpu.make_async_copy(staged.at[at], targets[at], out_sem.at[at]))
            outs[-1].start()
    for out in outs:
        out.wait()


def down_kernel(number, count, place_ref, experts_ref, hidden_ref, w_down, *refs):
    terms = refs[:count]
    expert = experts_ref[number]
    hidden, downs, staged, down_sem, out_sem, hidden_sem = refs[-6:]
    late = staged.shape[0]

    def down_copy(index):
        return down_piece(expert, w_down, downs, down_sem, place_ref[0], index, late + index, 0)

    hidden_copy = pltpu.make_async_copy(hidden_ref, hidden, hidden_sem)
    hidden_copy.start()
    if count:
        late_out, low_out, high_out, kept, summed, term_sem, sum_sem = refs[-13:-6]
        copies = [
            pltpu.make_async_copy(terms[index], kept.at[index], term_sem.at[index])
            for index in range(count)
        ]
        for copy in copies:
            copy.start()
    else:
        late_out = refs[-7]
    for index in range(late):
        down_copy(index).start()
    outs = []
    if count:
        for copy in copies:
            copy.wait()
        total = kept[0].astype(F32)
        for index in range(1, count):
            total += kept[index].astype(F32)
        summed[...] = total.astype(BF16)
        for index, out_ref in enumerate((low_out, high_out)):
            rows = pl.ds(index * CAP, CAP)
            outs.append(pltpu.make_async_copy(summed.at[rows], out_ref, sum_sem.at[index]))
            outs[-1].start()
    hidden_copy.wait()
    targets = [late_out.at[index] for index in range(late)]
    finish_down(targets, hidden, downs, staged, down_copy, out_sem)
    for out in outs:
        out.wait()


def expand(number, experts, rows, start, pieces, place, norm_gain, w_gate, w_up, w_down, after=()):
    cols = len(pieces)
    features, units = w_gate.shape[1], w_gate.shape[2]
    width, half = features // cols, cols // 2
    tile = 256 if units % 256 == 0 else 128
    anywhere = pl.BlockSpec(memory_space=pl.ANY)
    downs = half + half // 2
    weights = 2 * features * units + downs * units * width
    return pl.pallas_call(
        functools.partial(up_kernel, number, start, cols),
        out_shape=[
            jax.ShapeDtypeStruct((half, rows, width), BF16),
            jax.ShapeDtypeStruct((half // 2, rows, width), BF16),
            jax.ShapeDtypeStruct((rows, units), BF16),
        ],
        in_specs=[
            pl.BlockSpec(memory_space=pltpu.SMEM),
            pl.BlockSpec(memory_space=pltpu.SMEM),
            pl.BlockSpec(memory_space=pltpu.VMEM),
        ]
        + [anywhere] * (cols + 3 + len(after)),
        out_specs=[anywhere, anywhere, anywhere],
        scratch_shapes=[
            pltpu.VMEM((cols, rows, width), BF16),
            pltpu.VMEM((rows, features), BF16),
            pltpu.VMEM((SLOTS, features, 2 * tile), BF16),
            pltpu.VMEM((downs // 2, units, 2 * width), BF16),
            pltpu.VMEM((rows, units), BF16),
            pltpu.VMEM((downs, rows, width), BF16),
            pltpu.VMEM((rows, 2 * tile), F32),
            pltpu.VMEM((rows, 128), F32),
            pltpu.SemaphoreType.DMA((cols,)),
            pltpu.SemaphoreType.DMA((SLOTS,)),
            pltpu.SemaphoreType.DMA((SLOTS,)),
            pltpu.SemaphoreType.DMA((downs,)),
            pltpu.SemaphoreType.DMA((downs,)),
            pltpu.SemaphoreType.DMA,
        ],
        compiler_params=pltpu.CompilerParams(vmem_limit_bytes=VMEM),
        cost_estimate=pl.CostEstimate(
            flops=2 * rows * weights, bytes_accessed=2 * weights, transcendentals=rows * units
        ),
        name="expand",
    )(place, experts, norm_gain.reshape(cols, 1, width), *pieces, w_gate, w_up, w_down, *after)


def contract(number, experts, hidden, cols, place, w_down, terms=(), after=()):
    rows, units = hidden.shape
    width, late, count = w_down.shape[2] // cols, cols // 4, len(terms)
    anywhere = pl.BlockSpec(memory_space=pl.ANY)
    weights = units * width * late
    block = jax.ShapeDtypeStruct((CAP, width), BF16)
    side = [
        pltpu.VMEM((count, 2 * CAP, width), BF16),
        pltpu.VMEM((2 * CAP, width), BF16),
        pltpu.SemaphoreType.DMA((count,)),
        pltpu.SemaphoreType.DMA((2,)),
    ]
    out_shape = [jax.ShapeDtypeStruct((late, rows, width), BF16)] + [block, block] * bool(count)
    return pl.pallas_call(
        functools.partial(down_kernel, number, count),
        out_shape=out_shape,
        in_specs=[pl.BlockSpec(memory_space=pltpu.SMEM)] * 2 + [anywhere] * (2 + count + len(after)),
        out_specs=[anywhere] * len(out_shape),
        scratch_shapes=side * bool(count)
        + [
            pltpu.VMEM((rows, units), BF16),
            pltpu.VMEM((late // 2, units, 2 * width), BF16),
            pltpu.VMEM((late, rows, width), BF16),
            pltpu.SemaphoreType.DMA((late,)),
            pltpu.SemaphoreType.DMA((late,)),
            pltpu.SemaphoreType.DMA,
        ],
        compiler_params=pltpu.CompilerParams(vmem_limit_bytes=VMEM),
        cost_estimate=pl.CostEstimate(
            flops=128 * rows * weights, bytes_accessed=128 * weights, transcendentals=0
        ),
        name="contract",
    )(place, experts, hidden, w_down, *terms, *after)


def hold(arrays, after):
    anywhere = pl.BlockSpec(memory_space=pl.ANY)
    return pl.pallas_call(
        lambda *refs: None,
        out_shape=[jax.ShapeDtypeStruct(array.shape, array.dtype) for array in arrays],
        in_specs=[anywhere] * (len(arrays) + len(after)),
        out_specs=[anywhere] * len(arrays),
        input_output_aliases={i: i for i in range(len(arrays))},
        compiler_params=pltpu.CompilerParams(vmem_limit_bytes=VMEM),
        name="hold",
    )(*arrays, *after)


def pair_kernel(early_ref, late_ref, other_ref, *refs):
    half = other_ref.shape[0]
    out_refs = refs[:half]
    mine, other, staged, mine_sem, other_sem, out_sem = refs[half:]
    copies = []
    for index in range(half):
        source, at = (early_ref, index) if index < half // 2 else (late_ref, index - half // 2)
        copies.append(
            (
                pltpu.make_async_copy(source.at[at], mine.at[index], mine_sem.at[index]),
                pltpu.make_async_copy(other_ref.at[index], other.at[index], other_sem.at[index]),
            )
        )
    for ours, theirs in copies:
        ours.start()
        theirs.start()
    outs = []
    for index in range(half):
        for copy in copies[index]:
            copy.wait()
        both = mine[index].astype(F32) + other[index].astype(F32)
        staged[index] = both.astype(BF16)
        outs.append(pltpu.make_async_copy(staged.at[index], out_refs[index], out_sem.at[index]))
        outs[-1].start()
    for out in outs:
        out.wait()


def pair_sums(early, late, other):
    half, block = other.shape[0], other.shape[1:]
    anywhere = pl.BlockSpec(memory_space=pl.ANY)
    return pl.pallas_call(
        pair_kernel,
        out_shape=[jax.ShapeDtypeStruct(block, BF16)] * half,
        in_specs=[anywhere] * 3,
        out_specs=[anywhere] * half,
        scratch_shapes=[pltpu.VMEM(other.shape, BF16)] * 3 + [pltpu.SemaphoreType.DMA((half,))] * 3,
        compiler_params=pltpu.CompilerParams(vmem_limit_bytes=VMEM),
        name="pair_sums",
    )(early, late, other)


def add_kernel(count, *refs):
    terms, out_refs = refs[:count], refs[-2:]
    total = terms[0][...].astype(F32)
    for term in terms[1:]:
        total += term[...].astype(F32)
    for index, out_ref in enumerate(out_refs):
        out_ref[...] = total[index * CAP : (index + 1) * CAP].astype(BF16)


def add(terms):
    vmem = pl.BlockSpec(memory_space=pltpu.VMEM)
    block = jax.ShapeDtypeStruct((CAP, terms[0].shape[1]), BF16)
    return pl.pallas_call(
        functools.partial(add_kernel, len(terms)),
        out_shape=[block, block],
        in_specs=[vmem] * len(terms),
        out_specs=[vmem, vmem],
        compiler_params=pltpu.CompilerParams(vmem_limit_bytes=VMEM),
        name="add",
    )(*terms)


def movers(rows, cols):
    def along_row(value, relative):
        if relative == 0:
            return value
        return lax.ppermute(value, "row", [(i, i ^ relative) for i in range(rows)])

    def along_col(value, relative):
        if relative == 0:
            return value
        return lax.ppermute(value, "col", [(i, i ^ relative) for i in range(cols)])

    def gather(shares):
        return [along_col(shares, q) for q in range(0, cols, 2)]

    def complete(same_core):
        other_core = [along_col(piece, 1) for piece in same_core]
        return [piece for pair in zip(same_core, other_core) for piece in pair]

    return along_row, along_col, gather, complete


def body_one(rows, cols, tokens, norm_gain, expert_ids, gate_weights, w_gate, w_up, w_down):
    along_row, along_col, gather, complete = movers(rows, cols)
    row, place = lax.axis_index("row"), lax.axis_index("col").reshape(1)
    base = row.reshape(1)
    ids, token_weights = expert_ids.T, gate_weights.T
    experts = jnp.zeros((1,), jnp.int32)
    packed = pack([[k] for k in range(rows)], base, ids, tokens)
    arrived = [along_row(packed[k], k) for k in range(rows)]
    returned, pairs = [], []
    for first in range(0, rows, 2):
        shares = stack([[(0, 0), (1, 0)]], arrived[first : first + 2], experts)[0]
        pieces = complete(gather(shares.reshape(2 * CAP, -1)))
        send, early, hidden = expand(
            0, experts, 2 * CAP, 0, pieces, place, norm_gain, w_gate, w_up, w_down, after=pairs
        )
        got = along_col(send, 1)
        late = contract(0, experts, hidden, cols, place, w_down)[0]
        pairs = pair_sums(early, late, got)
        totals = add([along_col(share, 2 * q) for q, share in enumerate(pairs)])
        returned += [along_row(total, first + block) for block, total in enumerate(totals)]
    return combine(range(rows), [], base, base, ids, token_weights, tokens, returned, BF16)[0]


def body_two(rows, cols, tokens, norm_gain, expert_ids, gate_weights, w_gate, w_up, w_down):
    along_row, along_col, gather, complete = movers(rows, cols)
    row, place = lax.axis_index("row"), lax.axis_index("col").reshape(1)
    base = (row * 2).reshape(1)
    ids, token_weights = expert_ids.T, gate_weights.T
    packed = pack([[2 * k, 2 * k + 1] for k in range(rows)], base, ids, tokens)
    arrived = [along_row(packed[k], k) for k in range(rows)]
    all_ids = [along_row(ids, k) for k in range(rows)]
    busy, flips, starts, spill, near = plan(rows, 2, base, all_ids, arrived[:2])
    weights = (place, norm_gain, w_gate, w_up, w_down)

    def reduce(number, send, early, hidden, terms, after):
        got = along_col(send, 1)
        late, *more = contract(
            number, busy, hidden, cols, place, w_down, terms=terms, after=after
        )
        pairs = pair_sums(early, late, got)
        return pairs, [along_col(share, 2 * q) for q, share in enumerate(pairs)], more

    joined, rest = join(busy, starts, arrived)
    parts = gather(joined)
    pieces = complete(gather(near))
    send, early, hidden = expand(0, busy, 2 * CAP, 0, pieces, *weights, after=[joined])
    pairs, terms, _ = reduce(0, send, early, hidden, (), ())
    pieces = complete(hold(parts, pairs[:1]))
    returned, home = {}, []
    for chunk in range(1, rows // 2 + 1):
        start = 2 * CAP * (chunk - 1)
        size, number = (2 * CAP, 0) if chunk < rows // 2 else (MAIN, 1)
        send, early, hidden = expand(number, busy, size, start, pieces, *weights, after=pairs)
        pairs, next_terms, totals = reduce(number, send, early, hidden, terms, home)
        home = []
        for k, total in zip((2 * chunk - 2, 2 * chunk - 1), totals):
            returned[2 * k] = along_row(total, k)
            home.append(returned[2 * k])
        terms = next_terms

    def extra(last):
        pieces = complete(gather(rest))
        send, early, hidden = expand(1, busy, rest.shape[0], 0, pieces, *weights, after=[last])
        _, terms, _ = reduce(1, send, early, hidden, (), ())
        total = terms[0].astype(F32)
        for term in terms[1:]:
            total += term.astype(F32)
        return total.astype(BF16)

    more = lax.cond(spill[0] > MAIN, extra, lambda _: jnp.zeros(rest.shape, BF16), pairs[0])
    numbers, last = sorted(returned), [2 * k + 1 for k in range(rows)]
    slots = [returned[number] for number in numbers]
    partial, *pickers = combine(
        numbers, last, base, flips, ids, token_weights, tokens, slots, F32
    )
    totals = loosen(rows, starts, spill, more, terms)
    slots = [along_row(total, k) for k, total in enumerate(totals)]
    return finish(partial, pickers, slots)


def solution(mesh):
    placed = (
        P("row", "col"),
        P(),
        P("row", None),
        P("row", None),
        P("row", None, "col"),
        P("row", None, "col"),
        P("row", "col", None),
    )
    body = body_two if EXPERTS == 2 * mesh.shape["row"] else body_one
    return jax.shard_map(
        functools.partial(body, mesh.shape["row"], mesh.shape["col"]),
        mesh=mesh,
        in_specs=placed,
        out_specs=P("row", "col"),
        check_vma=False,
    )
```

```python
import functools
import jax
import jax.numpy as jnp
from jax import lax
from jax.experimental import pallas as pl
from jax.experimental.pallas import tpu as pltpu
from jax.sharding import PartitionSpec as P

EXPERTS = 8
CAP = 128
TOK_ROW = 256
MAIN = 336
SLOTS = 4
F32 = jnp.float32
BF16 = jnp.bfloat16
VMEM = 64 * 1024 * 1024
LITTLE = 16 * 1024 * 1024


def pack_kernel(chosen, base_ref, ids_ref, tokens_ref, *out_refs):
    tokens = tokens_ref.shape[0]
    numbers = lax.broadcasted_iota(jnp.int32, (EXPERTS, tokens), 0)
    ids = jnp.bitwise_xor(ids_ref[...], base_ref[0])
    hit = (numbers == ids[0:1, :]) | (numbers == ids[1:2, :])
    hits = jnp.where(hit, 1.0, 0.0)
    before = lax.broadcasted_iota(jnp.int32, (tokens, tokens), 0)
    after = lax.broadcasted_iota(jnp.int32, (tokens, tokens), 1)
    upper = jnp.where(before < after, 1.0, 0.0).astype(BF16)
    ranks = jnp.dot(hits.astype(BF16), upper, preferred_element_type=F32)
    ranks = jnp.where(hit, ranks, -1.0)
    slots = lax.broadcasted_iota(jnp.int32, (CAP, tokens), 0).astype(F32)
    for out_ref, experts in zip(out_refs, chosen):
        for index, expert in enumerate(experts):
            picker = jnp.where(slots == ranks[expert : expert + 1, :], 1.0, 0.0).astype(BF16)
            rows = jnp.dot(picker, tokens_ref[...], preferred_element_type=F32)
            out_ref[index] = rows.astype(BF16)


def pack(chosen, base, ids, tokens):
    width = tokens.shape[1]
    vmem = pl.BlockSpec(memory_space=pltpu.VMEM)
    return pl.pallas_call(
        functools.partial(pack_kernel, chosen),
        out_shape=[jax.ShapeDtypeStruct((len(c), CAP, width), BF16) for c in chosen],
        in_specs=[pl.BlockSpec(memory_space=pltpu.SMEM), vmem, vmem],
        out_specs=[vmem] * len(chosen),
        compiler_params=pltpu.CompilerParams(vmem_limit_bytes=VMEM),
        name="pack",
    )(base, ids, tokens)


def stack_kernel(layout, count, *refs):
    sources, index_ref, out_refs = refs[:count], refs[count], refs[-len(layout) :]
    for out_ref, parts in zip(out_refs, layout):
        for index, (source, at) in enumerate(parts):
            out_ref[index] = sources[source][index_ref[at]]


def stack(layout, sources, indices):
    vmem = pl.BlockSpec(memory_space=pltpu.VMEM)
    block = sources[0].shape[1:]
    return pl.pallas_call(
        functools.partial(stack_kernel, layout, len(sources)),
        out_shape=[jax.ShapeDtypeStruct((len(parts),) + block, BF16) for parts in layout],
        in_specs=[vmem] * len(sources) + [pl.BlockSpec(memory_space=pltpu.SMEM)],
        out_specs=[vmem] * len(layout),
        compiler_params=pltpu.CompilerParams(vmem_limit_bytes=VMEM),
        name="stack",
    )(*sources, indices)


def plan_kernel(rows, local, base_ref, *refs):
    ids_refs, sources = refs[:rows], refs[rows : rows + 2]
    busy_ref, flips_ref, starts_ref, spill_ref, shares_ref = refs[rows + 2 :]
    numbers = lax.broadcasted_iota(jnp.int32, (EXPERTS, TOK_ROW), 0)
    counts = []
    for ids_ref in ids_refs:
        ids = jnp.bitwise_xor(ids_ref[...], base_ref[0])
        hit = (numbers == ids[0:1, :]) | (numbers == ids[1:2, :])
        counts.append(jnp.sum(jnp.where(hit, 1.0, 0.0), axis=1, keepdims=True))
    loads = counts[0]
    for count in counts[1:]:
        loads += count

    def scalar(column, expert):
        return jnp.sum(column[expert : expert + 1, :]).astype(jnp.int32)

    spill = 0
    for k in range(rows):
        first, second = scalar(loads, 2 * k), scalar(loads, 2 * k + 1)
        flip = jnp.where(second > first, 1, 0)
        flips_ref[k] = flip
        spill = jnp.maximum(spill, jnp.minimum(first, second))
        if k == 0:
            small_is_first = flip
            for index, source in enumerate(sources):
                shares_ref[index * CAP : (index + 1) * CAP] = source[flip]
            busy_ref[0] = flip
            busy_ref[1] = 1 - flip
    spill_ref[0] = spill
    start = 0
    for k in range(rows):
        starts_ref[k] = start
        first, second = scalar(counts[k], 0), scalar(counts[k], 1)
        start = start + jnp.where(small_is_first == 1, first, second)
    starts_ref[rows] = start


def plan(rows, local, base, all_ids, sources):
    smem = pl.BlockSpec(memory_space=pltpu.SMEM)
    vmem = pl.BlockSpec(memory_space=pltpu.VMEM)
    sizes = [local, rows, rows + 1, 1]
    return pl.pallas_call(
        functools.partial(plan_kernel, rows, local),
        out_shape=[jax.ShapeDtypeStruct((size,), jnp.int32) for size in sizes]
        + [jax.ShapeDtypeStruct((2 * CAP, sources[0].shape[2]), BF16)],
        in_specs=[smem] + [vmem] * (rows + 2),
        out_specs=[smem] * 4 + [vmem],
        compiler_params=pltpu.CompilerParams(vmem_limit_bytes=VMEM),
        name="plan",
    )(base, *all_ids, *sources)


def join_kernel(busy_ref, starts_ref, *refs):
    sources, joined_ref, rest_ref = refs[:-2], refs[-2], refs[-1]
    far = (len(sources) - 2) * CAP
    for index, source in enumerate(sources[2:]):
        joined_ref[index * CAP : (index + 1) * CAP] = source[busy_ref[0]]
    for out_ref, at_row, size, begin in (
        (joined_ref, far, MAIN, 0),
        (rest_ref, 0, rest_ref.shape[0], MAIN),
    ):
        slot = lax.broadcasted_iota(jnp.int32, (size, CAP), 0) + begin
        rank = lax.broadcasted_iota(jnp.int32, (size, CAP), 1)
        total = jnp.zeros((size, out_ref.shape[1]), F32)
        for k, source in enumerate(sources):
            at = rank + starts_ref[k]
            picker = jnp.where((slot == at) & (at < starts_ref[k + 1]), 1.0, 0.0).astype(BF16)
            total += jnp.dot(picker, source[busy_ref[1]], preferred_element_type=F32)
        out_ref[at_row : at_row + size] = total.astype(BF16)


def join(busy, starts, sources):
    smem = pl.BlockSpec(memory_space=pltpu.SMEM)
    vmem = pl.BlockSpec(memory_space=pltpu.VMEM)
    rows, width = len(sources), sources[0].shape[2]
    sizes = [(rows - 2) * CAP + MAIN, rows * CAP - MAIN]
    return pl.pallas_call(
        join_kernel,
        out_shape=[jax.ShapeDtypeStruct((size, width), BF16) for size in sizes],
        in_specs=[smem] * 2 + [vmem] * rows,
        out_specs=[vmem] * 2,
        compiler_params=pltpu.CompilerParams(vmem_limit_bytes=VMEM),
        name="join",
    )(busy, starts, *sources)


def loosen_kernel(rows, starts_ref, spill_ref, rest_ref, *refs):
    terms, out_refs = refs[:-rows], refs[-rows:]
    total = terms[0][...].astype(F32)
    for term in terms[1:]:
        total += term[...].astype(F32)
    total = total.astype(BF16)
    main = total.shape[0]

    def place_rows(part, begin):
        slot = lax.broadcasted_iota(jnp.int32, (CAP, part.shape[0]), 1) + begin
        rank = lax.broadcasted_iota(jnp.int32, (CAP, part.shape[0]), 0)
        for k in range(rows):
            at = rank + starts_ref[k]
            picker = jnp.where((slot == at) & (at < starts_ref[k + 1]), 1.0, 0.0).astype(BF16)
            yield jnp.dot(picker, part, preferred_element_type=F32).astype(BF16)

    for out_ref, out in zip(out_refs, place_rows(total, 0)):
        out_ref[...] = out

    @pl.when(spill_ref[0] > main)
    def _():
        for out_ref, out in zip(out_refs, place_rows(rest_ref[...], main)):
            out_ref[...] += out


def loosen(rows, starts, spill, rest, terms):
    vmem = pl.BlockSpec(memory_space=pltpu.VMEM)
    block = jax.ShapeDtypeStruct((CAP, rest.shape[1]), BF16)
    return pl.pallas_call(
        functools.partial(loosen_kernel, rows),
        out_shape=[block] * rows,
        in_specs=[pl.BlockSpec(memory_space=pltpu.SMEM)] * 2 + [vmem] * (1 + len(terms)),
        out_specs=[vmem] * rows,
        compiler_params=pltpu.CompilerParams(vmem_limit_bytes=LITTLE),
        name="loosen",
    )(starts, spill, rest, *terms)


def combine_kernel(experts, later, count, base_ref, flips_ref, ids_ref, weights_ref, start_ref, *refs):
    slot_refs, out_ref, later_refs = refs[: len(experts)], refs[len(experts)], refs[len(experts) + 1 :]
    tokens = start_ref.shape[0]
    ids = jnp.bitwise_xor(ids_ref[...], base_ref[0])
    for k in range(count):
        ids = jnp.where(ids // 2 == k, jnp.bitwise_xor(ids, flips_ref[k]), ids)
    ids = ids.astype(F32)
    filler = jnp.zeros((4, tokens), F32)
    columns = jnp.transpose(jnp.concatenate([ids, weights_ref[...], filler], axis=0))
    lanes = lax.broadcasted_iota(jnp.int32, (tokens, 128), 1).astype(F32)
    first, second = columns[:, 0:1], columns[:, 1:2]
    hits = jnp.where((lanes == first) | (lanes == second), 1.0, 0.0)
    row = lax.broadcasted_iota(jnp.int32, (tokens, tokens), 0)
    column = lax.broadcasted_iota(jnp.int32, (tokens, tokens), 1)
    lower = jnp.where(column < row, 1.0, 0.0).astype(BF16)
    ranks = jnp.dot(lower, hits.astype(BF16), preferred_element_type=F32)
    total = start_ref[...].astype(F32)
    for choice, chosen in enumerate((first, second)):
        rank = jnp.sum(jnp.where(lanes == chosen, ranks, 0.0), axis=1, keepdims=True)
        matches = jnp.where(lanes == rank, 1.0, 0.0)
        picked = jnp.zeros(total.shape, F32)
        for expert, slot_ref in zip(experts, slot_refs):
            picker = jnp.where(chosen == expert, matches, 0.0).astype(BF16)
            picked += jnp.dot(picker, slot_ref[...], preferred_element_type=F32)
        total += picked * columns[:, 2 + choice : 3 + choice]
        for index, expert in enumerate(later):
            picker = jnp.where(chosen == expert, matches, 0.0).astype(BF16)
            later_refs[choice][:, index * CAP : (index + 1) * CAP] = picker
    out_ref[...] = total.astype(out_ref.dtype)
    if later:
        later_refs[2][...] = columns


def combine(experts, later, base, flips, ids, gate_weights, start, slots, kind):
    tokens = start.shape[0]
    pickers = [jax.ShapeDtypeStruct((tokens, CAP * len(later)), BF16)] * 2
    extra = pickers + [jax.ShapeDtypeStruct((tokens, 8), F32)] if later else []
    count = flips.shape[0] if EXPERTS == 2 * flips.shape[0] else 0
    vmem = pl.BlockSpec(memory_space=pltpu.VMEM)
    return pl.pallas_call(
        functools.partial(combine_kernel, experts, later, count),
        out_shape=[jax.ShapeDtypeStruct(start.shape, kind)] + extra,
        in_specs=[pl.BlockSpec(memory_space=pltpu.SMEM)] * 2 + [vmem] * (3 + len(slots)),
        out_specs=[vmem] * (1 + len(extra)),
        compiler_params=pltpu.CompilerParams(vmem_limit_bytes=LITTLE),
        name="combine",
    )(base, flips, ids, gate_weights, start, *slots)


def finish_kernel(start_ref, first_ref, second_ref, columns_ref, *refs):
    slot_refs, out_ref = refs[:-1], refs[-1]
    total = start_ref[...]
    for choice, picker_ref in enumerate((first_ref, second_ref)):
        picked = jnp.zeros(total.shape, F32)
        for index, slot_ref in enumerate(slot_refs):
            picker = picker_ref[:, index * CAP : (index + 1) * CAP]
            picked += jnp.dot(picker, slot_ref[...], preferred_element_type=F32)
        total += picked * columns_ref[:, 2 + choice : 3 + choice]
    out_ref[...] = total.astype(out_ref.dtype)


def finish(start, pickers, slots):
    vmem = pl.BlockSpec(memory_space=pltpu.VMEM)
    return pl.pallas_call(
        finish_kernel,
        out_shape=jax.ShapeDtypeStruct(start.shape, BF16),
        in_specs=[vmem] * (1 + len(pickers) + len(slots)),
        out_specs=vmem,
        compiler_params=pltpu.CompilerParams(vmem_limit_bytes=LITTLE),
        name="finish",
    )(start, *pickers, *slots)


def up_kernel(number, start, cols, place_ref, experts_ref, gain_ref, *refs):
    count = cols
    expert = experts_ref[number]
    pieces = refs[:count]
    w_gate, w_up, w_down = refs[count : count + 3]
    (send_out, early_out, hidden_out, raw, scaled, ups, downs, hidden, staged, total, squares) = refs[-17:-6]
    x_sem, gate_sem, up_sem, down_sem, out_sem, hidden_sem = refs[-6:]
    slots, features = ups.shape[0], ups.shape[1]
    tile, units, width = ups.shape[2] // 2, hidden.shape[1], raw.shape[2]
    tiles, half = units // tile, cols // 2
    place = place_ref[0]

    def up_copies(index):
        slot = lax.rem(index, slots)
        columns = pl.ds(pl.multiple_of(index * tile, tile), tile)
        return (
            pltpu.make_async_copy(
                w_gate.at[expert, :, columns], ups.at[slot, :, pl.ds(0, tile)], gate_sem.at[slot]
            ),
            pltpu.make_async_copy(
                w_up.at[expert, :, columns], ups.at[slot, :, pl.ds(tile, tile)], up_sem.at[slot]
            ),
        )

    def down_copy(index):
        core, at = (1, index) if index < half else (0, index - half)
        return down_piece(expert, w_down, downs, down_sem, place, index, at, core)

    def piece_copy(relative):
        rows = pl.ds(start, raw.shape[1])
        return pltpu.make_async_copy(
            pieces[relative].at[rows], raw.at[relative], x_sem.at[relative]
        )

    for relative in range(cols):
        piece_copy(relative).start()
    for copy in up_copies(0):
        copy.start()
    for relative in range(cols):
        piece_copy(relative).wait()
        values = raw[relative].astype(F32)
        square = values * values
        part = square[:, 0:128]
        for lane in range(128, width, 128):
            part += square[:, lane : lane + 128]
        if relative == 0:
            squares[...] = part
        else:
            squares[...] += part
    for index in range(1, slots):
        for copy in up_copies(index):
            copy.start()
    mean = jnp.sum(squares[...], axis=1, keepdims=True) * (1.0 / features)
    inverse = lax.rsqrt(mean + 1e-05)
    for copy in up_copies(0):
        copy.wait()
    for relative in range(cols):
        owner = jnp.bitwise_xor(place, relative)
        at = pl.ds(pl.multiple_of(owner * width, width), width)
        share = (raw[relative].astype(F32) * inverse * gain_ref[owner]).astype(BF16)
        scaled[:, at] = share
        product = jnp.dot(share, ups[0, at, :], preferred_element_type=F32)
        if relative == 0:
            total[...] = product
        else:
            total[...] += product

    def activate(both, columns):
        gate, up = both[:, :tile], both[:, tile:]
        hidden[:, columns] = (gate / (1.0 + jnp.exp(-gate)) * up).astype(BF16)

    activate(total[...], pl.ds(0, tile))

    @pl.loop(1, tiles)
    def _(index):
        for copy in up_copies(index):
            copy.wait()

        @pl.when(index + slots - 1 < tiles)
        def _():
            for copy in up_copies(index + slots - 1):
                copy.start()

        for step in range(half + half // 2):

            @pl.when(index == tiles - slots + 1 + step * (slots - 1) // (half + half // 2))
            def _():
                down_copy(step).start()

        both = jnp.dot(scaled[...], ups[lax.rem(index, slots)], preferred_element_type=F32)
        activate(both, pl.ds(pl.multiple_of(index * tile, tile), tile))

    hidden_copy = pltpu.make_async_copy(hidden, hidden_out, hidden_sem)
    hidden_copy.start()
    targets = [send_out.at[index] for index in range(half)]
    targets += [early_out.at[index] for index in range(half // 2)]
    finish_down(targets, hidden, downs, staged, down_copy, out_sem)
    hidden_copy.wait()


def down_piece(expert, w_down, downs, down_sem, place, slot, index, core):
    width = downs.shape[2] // 2
    owner = jnp.bitwise_xor(place, 2 * index + core)
    return pltpu.make_async_copy(
        w_down.at[expert, :, pl.ds(pl.multiple_of(owner * width, width), width)],
        downs.at[slot // 2, :, pl.ds(slot % 2 * width, width)],
        down_sem.at[slot],
    )


def finish_down(targets, hidden, downs, staged, down_copy, out_sem):
    outs = []
    width = downs.shape[2] // 2
    for index in range(0, len(targets), 2):
        down_copy(index).wait()
        down_copy(index + 1).wait()
        both = jnp.dot(hidden[...], downs[index // 2], preferred_element_type=F32).astype(BF16)
        for at in (index, index + 1):
            start = (at - index) * width
            staged[at] = both[:, start : start + width]
            outs.append(pltpu.make_async_copy(staged.at[at], targets[at], out_sem.at[at]))
            outs[-1].start()
    for out in outs:
        out.wait()


def down_kernel(number, count, place_ref, experts_ref, hidden_ref, w_down, *refs):
    terms = refs[:count]
    expert = experts_ref[number]
    hidden, downs, staged, down_sem, out_sem, hidden_sem = refs[-6:]
    late = staged.shape[0]

    def down_copy(index):
        return down_piece(expert, w_down, downs, down_sem, place_ref[0], index, late + index, 0)

    hidden_copy = pltpu.make_async_copy(hidden_ref, hidden, hidden_sem)
    hidden_copy.start()
    if count:
        late_out, low_out, high_out, kept, summed, term_sem, sum_sem = refs[-13:-6]
        copies = [
            pltpu.make_async_copy(terms[index], kept.at[index], term_sem.at[index])
            for index in range(count)
        ]
        for copy in copies:
            copy.start()
    else:
        late_out = refs[-7]
    for index in range(late):
        down_copy(index).start()
    outs = []
    if count:
        for copy in copies:
            copy.wait()
        total = kept[0].astype(F32)
        for index in range(1, count):
            total += kept[index].astype(F32)
        summed[...] = total.astype(BF16)
        for index, out_ref in enumerate((low_out, high_out)):
            rows = pl.ds(index * CAP, CAP)
            outs.append(pltpu.make_async_copy(summed.at[rows], out_ref, sum_sem.at[index]))
            outs[-1].start()
    hidden_copy.wait()
    targets = [late_out.at[index] for index in range(late)]
    finish_down(targets, hidden, downs, staged, down_copy, out_sem)
    for out in outs:
        out.wait()


def expand(number, experts, rows, start, pieces, place, norm_gain, w_gate, w_up, w_down, after=()):
    cols = len(pieces)
    features, units = w_gate.shape[1], w_gate.shape[2]
    width, half = features // cols, cols // 2
    tile = 256 if units % 256 == 0 else 128
    anywhere = pl.BlockSpec(memory_space=pl.ANY)
    downs = half + half // 2
    weights = 2 * features * units + downs * units * width
    return pl.pallas_call(
        functools.partial(up_kernel, number, start, cols),
        out_shape=[
            jax.ShapeDtypeStruct((half, rows, width), BF16),
            jax.ShapeDtypeStruct((half // 2, rows, width), BF16),
            jax.ShapeDtypeStruct((rows, units), BF16),
        ],
        in_specs=[
            pl.BlockSpec(memory_space=pltpu.SMEM),
            pl.BlockSpec(memory_space=pltpu.SMEM),
            pl.BlockSpec(memory_space=pltpu.VMEM),
        ]
        + [anywhere] * (cols + 3 + len(after)),
        out_specs=[anywhere, anywhere, anywhere],
        scratch_shapes=[
            pltpu.VMEM((cols, rows, width), BF16),
            pltpu.VMEM((rows, features), BF16),
            pltpu.VMEM((SLOTS, features, 2 * tile), BF16),
            pltpu.VMEM((downs // 2, units, 2 * width), BF16),
            pltpu.VMEM((rows, units), BF16),
            pltpu.VMEM((downs, rows, width), BF16),
            pltpu.VMEM((rows, 2 * tile), F32),
            pltpu.VMEM((rows, 128), F32),
            pltpu.SemaphoreType.DMA((cols,)),
            pltpu.SemaphoreType.DMA((SLOTS,)),
            pltpu.SemaphoreType.DMA((SLOTS,)),
            pltpu.SemaphoreType.DMA((downs,)),
            pltpu.SemaphoreType.DMA((downs,)),
            pltpu.SemaphoreType.DMA,
        ],
        compiler_params=pltpu.CompilerParams(vmem_limit_bytes=VMEM),
        cost_estimate=pl.CostEstimate(
            flops=2 * rows * weights, bytes_accessed=2 * weights, transcendentals=rows * units
        ),
        name="expand",
    )(place, experts, norm_gain.reshape(cols, 1, width), *pieces, w_gate, w_up, w_down, *after)


def contract(number, experts, hidden, cols, place, w_down, terms=(), after=()):
    rows, units = hidden.shape
    width, late, count = w_down.shape[2] // cols, cols // 4, len(terms)
    anywhere = pl.BlockSpec(memory_space=pl.ANY)
    weights = units * width * late
    block = jax.ShapeDtypeStruct((CAP, width), BF16)
    side = [
        pltpu.VMEM((count, 2 * CAP, width), BF16),
        pltpu.VMEM((2 * CAP, width), BF16),
        pltpu.SemaphoreType.DMA((count,)),
        pltpu.SemaphoreType.DMA((2,)),
    ]
    out_shape = [jax.ShapeDtypeStruct((late, rows, width), BF16)] + [block, block] * bool(count)
    return pl.pallas_call(
        functools.partial(down_kernel, number, count),
        out_shape=out_shape,
        in_specs=[pl.BlockSpec(memory_space=pltpu.SMEM)] * 2 + [anywhere] * (2 + count + len(after)),
        out_specs=[anywhere] * len(out_shape),
        scratch_shapes=side * bool(count)
        + [
            pltpu.VMEM((rows, units), BF16),
            pltpu.VMEM((late // 2, units, 2 * width), BF16),
            pltpu.VMEM((late, rows, width), BF16),
            pltpu.SemaphoreType.DMA((late,)),
            pltpu.SemaphoreType.DMA((late,)),
            pltpu.SemaphoreType.DMA,
        ],
        compiler_params=pltpu.CompilerParams(vmem_limit_bytes=VMEM),
        cost_estimate=pl.CostEstimate(
            flops=128 * rows * weights, bytes_accessed=128 * weights, transcendentals=0
        ),
        name="contract",
    )(place, experts, hidden, w_down, *terms, *after)


def hold(arrays, after):
    anywhere = pl.BlockSpec(memory_space=pl.ANY)
    return pl.pallas_call(
        lambda *refs: None,
        out_shape=[jax.ShapeDtypeStruct(array.shape, array.dtype) for array in arrays],
        in_specs=[anywhere] * (len(arrays) + len(after)),
        out_specs=[anywhere] * len(arrays),
        input_output_aliases={i: i for i in range(len(arrays))},
        compiler_params=pltpu.CompilerParams(vmem_limit_bytes=VMEM),
        name="hold",
    )(*arrays, *after)


def pair_kernel(early_ref, late_ref, other_ref, *refs):
    half = other_ref.shape[0]
    out_refs = refs[:half]
    mine, other, staged, mine_sem, other_sem, out_sem = refs[half:]
    copies = []
    for index in range(half):
        source, at = (early_ref, index) if index < half // 2 else (late_ref, index - half // 2)
        copies.append(
            (
                pltpu.make_async_copy(source.at[at], mine.at[index], mine_sem.at[index]),
                pltpu.make_async_copy(other_ref.at[index], other.at[index], other_sem.at[index]),
            )
        )
    for ours, theirs in copies:
        ours.start()
        theirs.start()
    outs = []
    for index in range(half):
        for copy in copies[index]:
            copy.wait()
        both = mine[index].astype(F32) + other[index].astype(F32)
        staged[index] = both.astype(BF16)
        outs.append(pltpu.make_async_copy(staged.at[index], out_refs[index], out_sem.at[index]))
        outs[-1].start()
    for out in outs:
        out.wait()


def pair_sums(early, late, other):
    half, block = other.shape[0], other.shape[1:]
    anywhere = pl.BlockSpec(memory_space=pl.ANY)
    return pl.pallas_call(
        pair_kernel,
        out_shape=[jax.ShapeDtypeStruct(block, BF16)] * half,
        in_specs=[anywhere] * 3,
        out_specs=[anywhere] * half,
        scratch_shapes=[pltpu.VMEM(other.shape, BF16)] * 3 + [pltpu.SemaphoreType.DMA((half,))] * 3,
        compiler_params=pltpu.CompilerParams(vmem_limit_bytes=VMEM),
        name="pair_sums",
    )(early, late, other)


def add_kernel(count, *refs):
    terms, out_refs = refs[:count], refs[-2:]
    total = terms[0][...].astype(F32)
    for term in terms[1:]:
        total += term[...].astype(F32)
    for index, out_ref in enumerate(out_refs):
        out_ref[...] = total[index * CAP : (index + 1) * CAP].astype(BF16)


def add(terms):
    vmem = pl.BlockSpec(memory_space=pltpu.VMEM)
    block = jax.ShapeDtypeStruct((CAP, terms[0].shape[1]), BF16)
    return pl.pallas_call(
        functools.partial(add_kernel, len(terms)),
        out_shape=[block, block],
        in_specs=[vmem] * len(terms),
        out_specs=[vmem, vmem],
        compiler_params=pltpu.CompilerParams(vmem_limit_bytes=VMEM),
        name="add",
    )(*terms)


def movers(rows, cols):
    def along_row(value, relative):
        if relative == 0:
            return value
        return lax.ppermute(value, "row", [(i, i ^ relative) for i in range(rows)])

    def along_col(value, relative):
        if relative == 0:
            return value
        return lax.ppermute(value, "col", [(i, i ^ relative) for i in range(cols)])

    def gather(shares):
        return [along_col(shares, q) for q in range(0, cols, 2)]

    def complete(same_core):
        other_core = [along_col(piece, 1) for piece in same_core]
        return [piece for pair in zip(same_core, other_core) for piece in pair]

    return along_row, along_col, gather, complete


def body_one(rows, cols, tokens, norm_gain, expert_ids, gate_weights, w_gate, w_up, w_down):
    along_row, along_col, gather, complete = movers(rows, cols)
    row, place = lax.axis_index("row"), lax.axis_index("col").reshape(1)
    base = row.reshape(1)
    ids, token_weights = expert_ids.T, gate_weights.T
    experts = jnp.zeros((1,), jnp.int32)
    packed = pack([[k] for k in range(rows)], base, ids, tokens)
    arrived = [along_row(packed[k], k) for k in range(rows)]
    returned, pairs = [], []
    for first in range(0, rows, 2):
        shares = stack([[(0, 0), (1, 0)]], arrived[first : first + 2], experts)[0]
        pieces = complete(gather(shares.reshape(2 * CAP, -1)))
        send, early, hidden = expand(
            0, experts, 2 * CAP, 0, pieces, place, norm_gain, w_gate, w_up, w_down, after=pairs
        )
        got = along_col(send, 1)
        late = contract(0, experts, hidden, cols, place, w_down)[0]
        pairs = pair_sums(early, late, got)
        totals = add([along_col(share, 2 * q) for q, share in enumerate(pairs)])
        returned += [along_row(total, first + block) for block, total in enumerate(totals)]
    return combine(range(rows), [], base, base, ids, token_weights, tokens, returned, BF16)[0]


def body_two(rows, cols, tokens, norm_gain, expert_ids, gate_weights, w_gate, w_up, w_down):
    along_row, along_col, gather, complete = movers(rows, cols)
    row, place = lax.axis_index("row"), lax.axis_index("col").reshape(1)
    base = (row * 2).reshape(1)
    ids, token_weights = expert_ids.T, gate_weights.T
    packed = pack([[2 * k, 2 * k + 1] for k in range(rows)], base, ids, tokens)
    arrived = [along_row(packed[k], k) for k in range(rows)]
    all_ids = [along_row(ids, k) for k in range(rows)]
    busy, flips, starts, spill, near = plan(rows, 2, base, all_ids, arrived[:2])
    weights = (place, norm_gain, w_gate, w_up, w_down)

    def reduce(number, send, early, hidden, terms, after):
        got = along_col(send, 1)
        late, *more = contract(
            number, busy, hidden, cols, place, w_down, terms=terms, after=after
        )
        pairs = pair_sums(early, late, got)
        return pairs, [along_col(share, 2 * q) for q, share in enumerate(pairs)], more

    joined, rest = join(busy, starts, arrived)
    parts = gather(joined)
    pieces = complete(gather(near))
    send, early, hidden = expand(0, busy, 2 * CAP, 0, pieces, *weights, after=[joined])
    pairs, terms, _ = reduce(0, send, early, hidden, (), ())
    pieces = complete(hold(parts, pairs[:1]))
    returned, home = {}, []
    for chunk in range(1, rows // 2 + 1):
        start = 2 * CAP * (chunk - 1)
        size, number = (2 * CAP, 0) if chunk < rows // 2 else (MAIN, 1)
        send, early, hidden = expand(number, busy, size, start, pieces, *weights, after=pairs)
        pairs, next_terms, totals = reduce(number, send, early, hidden, terms, home)
        home = []
        for k, total in zip((2 * chunk - 2, 2 * chunk - 1), totals):
            returned[2 * k] = along_row(total, k)
            home.append(returned[2 * k])
        terms = next_terms

    def extra(last):
        pieces = complete(gather(rest))
        send, early, hidden = expand(1, busy, rest.shape[0], 0, pieces, *weights, after=[last])
        _, terms, _ = reduce(1, send, early, hidden, (), ())
        total = terms[0].astype(F32)
        for term in terms[1:]:
            total += term.astype(F32)
        return total.astype(BF16)

    more = lax.cond(spill[0] > MAIN, extra, lambda _: jnp.zeros(rest.shape, BF16), pairs[0])
    numbers, last = sorted(returned), [2 * k + 1 for k in range(rows)]
    slots = [returned[number] for number in numbers]
    partial, *pickers = combine(
        numbers, last, base, flips, ids, token_weights, tokens, slots, F32
    )
    totals = loosen(rows, starts, spill, more, terms)
    slots = [along_row(total, k) for k, total in enumerate(totals)]
    return finish(partial, pickers, slots)


def solution(mesh):
    placed = (
        P("row", "col"),
        P(),
        P("row", None),
        P("row", None),
        P("row", None, "col"),
        P("row", None, "col"),
        P("row", "col", None),
    )
    body = body_two if EXPERTS == 2 * mesh.shape["row"] else body_one
    return jax.shard_map(
        functools.partial(body, mesh.shape["row"], mesh.shape["col"]),
        mesh=mesh,
        in_specs=placed,
        out_specs=P("row", "col"),
        check_vma=False,
    )
```
